32 devices in a mesh: dp: 2 (over core), wide: 16 (over z, y, x).
Axes of the slice: x: 2, y: 2, z: 4, core: 2. Of those that a mesh axis runs over, the one named last changes fastest.
Arguments:
- tokens: bfloat16 [32, 1024, 256], P(('dp', 'wide')), may hold values from -6 to 6
- item_lengths: int32 [32, 20], P(('dp', 'wide')), may hold values from 5 to 100, as said below
- loop_counts: int32 [32, 20], P(('dp', 'wide')), may hold values from 1 to 2
- w_query: bfloat16 [256, 256], P('wide'), may hold values from -0.5 to 0.5
- w_key: bfloat16 [256, 256], P('wide'), may hold values from -0.5 to 0.5
- w_value: bfloat16 [256, 256], P('wide'), may hold values from -0.375 to 0.375
- w_out: bfloat16 [256, 256], P(None, 'wide'), may hold values from -1.5 to 1.5
- w_up: bfloat16 [256, 1024], P('wide'), may hold values from -0.375 to 0.375
- w_down: bfloat16 [1024, 256], P(None, 'wide'), may hold values from -0.1875 to 0.1875
- gain_one: bfloat16 [256], P('wide'), may hold values from 0.25 to 1.75
- shift_one: bfloat16 [256], P('wide'), may hold values from -4 to 4
- gain_two: bfloat16 [256], P('wide'), may hold values from 0.25 to 1.75
- shift_two: bfloat16 [256], P('wide'), may hold values from -4 to 4
- bias_up: bfloat16 [1024], P('wide'), may hold values from -4 to 4
- bias_down: bfloat16 [256], P('wide'), may hold values from -4 to 4
- cotangent: bfloat16 [32, 1024, 256], P(('dp', 'wide')), may hold values from -6 to 6
Outputs:
- output: bfloat16 [32, 1024, 256], P(('dp', 'wide'))
- input_grad: bfloat16 [32, 1024, 256], P(('dp', 'wide'))
- grad_query: float32 [256, 256], P('wide')
- grad_key: float32 [256, 256], P('wide')
- grad_value: float32 [256, 256], P('wide')
- grad_out: float32 [256, 256], P(None, 'wide')
- grad_up: float32 [256, 1024], P('wide')
- grad_down: float32 [1024, 256], P(None, 'wide')
- grad_gain_one: float32 [256], P('wide')
- grad_shift_one: float32 [256], P('wide')
- grad_gain_two: float32 [256], P('wide')
- grad_shift_two: float32 [256], P('wide')
- grad_bias_up: float32 [1024], P('wide')
- grad_bias_down: float32 [256], P('wide')
The draws below stay inside these ranges and needn't reach their ends.
Inputs may be any that keep to these rules, and one draw needn't show every extreme that they name: `item_lengths`: in each row the 20 item lengths add up to 1024; each row has at least one item of exactly 100 slots and at least one of exactly 5.
All inputs are finite; a program needn't handle non-finite values.
Results may differ from the reference program's by a relative error of at most 0.017.
The reference program's roundings to bfloat16 on the way count: a program that leaves them out, or rounds other values in their place, can miss the bound.
Values may be sent and summed in bfloat16 or wider, within the bound.
A program may use at most 192 MiB of HBM per device.

```python
import jax
import jax.numpy as jnp
from jax import lax

D = 256
HEADS = 4
FF = 1024
SLOTS = 1024
ITEMS = 20
MINLEN = 5
MAXLEN = 100
LOOPS = 2
ROWS = 32


def draw_item_lengths(key, part):
    key = jax.random.fold_in(key, 11)
    pair_count = ITEMS // 2
    pair_total = MINLEN + MAXLEN
    last_total = SLOTS - (pair_count - 1) * pair_total
    key_first, key_last, key_order = jax.random.split(key, 3)
    first_len = jax.random.randint(key_first, (ROWS, pair_count), MINLEN, MAXLEN + 1)
    last_first = jax.random.randint(key_last, (ROWS,), MINLEN, last_total - MINLEN + 1)
    first_len = first_len.at[:, 0].set(MAXLEN)
    first_len = first_len.at[:, pair_count - 1].set(last_first)
    pair_sums = jnp.full((pair_count,), pair_total, dtype=jnp.int32).at[pair_count - 1].set(last_total)
    second_len = pair_sums[None, :] - first_len
    joined = jnp.stack([first_len, second_len], axis=2).reshape(ROWS, ITEMS)
    row_keys = jax.random.split(key_order, ROWS)
    orders = jax.vmap(lambda row_key: jax.random.permutation(row_key, ITEMS))(row_keys)
    return jnp.take_along_axis(joined, orders, axis=1).astype(jnp.int32)


def place_ends(array, stream_key, smallest, high):
    dims = array.shape
    spot = [jax.random.randint(jax.random.fold_in(stream_key, axis), (), 0, dims[axis]) for axis in range(len(dims))]
    array = array.at[tuple(spot)].set(smallest)
    longest = dims.index(max(dims))
    spot[longest] = (spot[longest] + 1) % dims[longest]
    return array.at[tuple(spot)].set(high)


def raised(result, own_key, source, target, blocks, factor):
    owner, partner = [(jnp.arange(result.shape[position]) // (result.shape[position] // blocks)).reshape([-1 if axis == position else 1 for axis in range(result.ndim)]) for position in (source, target)]
    chosen = jax.random.permutation(own_key, blocks)[partner]
    strong = (owner == chosen) | (owner == (partner + blocks // 2) % blocks)
    return jnp.where(strong, factor * result, result)


def levels(rng, shape, pieces, smallest, high):
    def one(axis_at, blocks):
        steps = jax.random.uniform(jax.random.fold_in(jax.random.fold_in(rng, 6), axis_at), (blocks,), jnp.float32, smallest / len(pieces), high / len(pieces))
        return jnp.repeat(jnp.exp(steps), shape[axis_at] // blocks).reshape((-1,) + (1,) * (len(shape) - axis_at - 1))

    level = one(*pieces[0])
    for cut in pieces[1:]:
        level = level * one(*cut)
    return level


def normal_values(key, shape, scale, limit, pieces=(), kind=jnp.bfloat16):
    level = levels(key, shape, pieces, -0.22, 0.18) if pieces else 1.0
    drawn = jax.random.normal(key, shape, jnp.float32) * scale * level
    return jnp.minimum(jnp.maximum(drawn, -limit), limit).astype(kind)


def gaussian_with(own_key, extent, deviation, bound, cuts, heavy, kind=jnp.bfloat16):
    result = deviation * jax.random.normal(own_key, extent, jnp.float32)
    if cuts:
        result = result * levels(own_key, extent, cuts, -0.22, 0.18)
    return jnp.clip(raised(result, jax.random.fold_in(own_key, 3), *heavy), -bound, bound).astype(kind)


def setup_inputs(seed: int = 0) -> dict:
    streams_of = jax.random.split(jax.random.key(seed), 17)
    return {
        "tokens": normal_values(streams_of[0], (ROWS, SLOTS, D), 1.0, 6.0, ((0, 32),)),
        "item_lengths": draw_item_lengths(jax.random.fold_in(streams_of[16], 71), 0),
        "loop_counts": place_ends(jax.random.randint(streams_of[2], (ROWS, ITEMS), 1, 3), jax.random.fold_in(streams_of[2], 1), 1, 2).astype(jnp.int32),
        "w_query": normal_values(streams_of[3], (D, D), (D // 2) ** -0.5, 0.5, ((0, 16),)),
        "w_key": normal_values(streams_of[4], (D, D), (D // 2) ** -0.5, 0.5, ((0, 16),)),
        "w_value": normal_values(streams_of[5], (D, D), D ** -0.5, 0.375, ((0, 16),)),
        "w_out": normal_values(streams_of[6], (D, D), (D // 16) ** -0.5, 1.5, ((1, 16),)),
        "w_up": normal_values(streams_of[7], (D, FF), D ** -0.5, 0.375, ((0, 16),)),
        "w_down": normal_values(streams_of[8], (FF, D), FF ** -0.5, 0.1875, ((1, 16),)),
        "gain_one": jnp.clip(1.0 + 0.15 * jax.random.normal(streams_of[9], (D,), jnp.float32), 0.25, 1.75).astype(jnp.bfloat16),
        "shift_one": normal_values(streams_of[10], (D,), 0.3, 4.0, ((0, 16),)),
        "gain_two": jnp.clip(1.0 + 0.15 * jax.random.normal(streams_of[11], (D,), jnp.float32), 0.25, 1.75).astype(jnp.bfloat16),
        "shift_two": normal_values(streams_of[12], (D,), 0.3, 4.0, ((0, 16),)),
        "bias_up": normal_values(streams_of[13], (FF,), 0.5, 4.0, ((0, 16),)),
        "bias_down": normal_values(streams_of[14], (D,), 0.3, 4.0, ((0, 16),)),
        "cotangent": gaussian_with(streams_of[15], (ROWS, SLOTS, D), 1.0, 6.0, ((0, 32),), (0, 2, 32, 2.75)),
    }


@jax.custom_vjp
def low(v):
    return lax.optimization_barrier(v.astype(jnp.bfloat16)).astype(jnp.float32)

@jax.custom_vjp
def low_back(v):
    return v

def low_keep(v):
    return (low(v), None)

def low_pass(kept, grad):
    return (grad,)

def back_keep(v):
    return (v, None)

def back_low(kept, grad):
    return (low(grad),)
low.defvjp(low_keep, low_pass)
low_back.defvjp(back_keep, back_low)
NORM_EPS = 1e-05
MASK_FILL = -1e+30
HIGHEST = lax.Precision.HIGHEST

def layer_norm(values, norm_gain, norm_shift):
    average = lax.optimization_barrier(jnp.mean(values, axis=-1, keepdims=True))
    centered = values - average
    spread = lax.optimization_barrier(jnp.mean(centered * centered, axis=-1, keepdims=True))
    return centered * lax.rsqrt(spread + NORM_EPS) * norm_gain + norm_shift

def gelu_tanh(values):
    return jax.nn.gelu(values, approximate=True)

def row_layout(lengths, counts):
    item_ends = jnp.cumsum(lengths).astype(jnp.int32)
    positions = jnp.arange(SLOTS, dtype=jnp.int32)
    item_of = lax.optimization_barrier(jnp.sum((item_ends[None, :] <= positions[:, None]).astype(jnp.int32), axis=1)).astype(jnp.int32)
    matches = item_of[:, None] == jnp.arange(ITEMS, dtype=jnp.int32)[None, :]
    loops_slot = lax.optimization_barrier(jnp.sum(jnp.where(matches, counts[None, :], 0), axis=1)).astype(jnp.int32)
    allowed = (item_of[:, None] == item_of[None, :]) & (positions[None, :] <= positions[:, None])
    return (loops_slot, allowed)

def block_forward(current, inputs, allowed, params):
    w_query, w_key, w_value, w_out, w_up, w_down, gain_one, shift_one, gain_two, shift_two, bias_up, bias_down = params
    head_dim = D // HEADS
    scaling = head_dim ** (-0.5)
    mixed_in = current + inputs
    normed = low(layer_norm(mixed_in, gain_one, shift_one))
    queries = low(low_back(jnp.dot(normed, w_query, precision=HIGHEST))).reshape(SLOTS, HEADS, head_dim)
    keys_act = low(low_back(jnp.dot(normed, w_key, precision=HIGHEST))).reshape(SLOTS, HEADS, head_dim)
    values_act = low(low_back(jnp.dot(normed, w_value, precision=HIGHEST))).reshape(SLOTS, HEADS, head_dim)
    scores = low_back(jnp.einsum('qhd,khd->hqk', queries, keys_act, precision=HIGHEST) * scaling)
    scores = jnp.where(allowed[None, :, :], scores, MASK_FILL)
    largest = lax.optimization_barrier(jnp.max(scores, axis=-1, keepdims=True))
    exponent = jnp.exp(scores - largest)
    attn_probs = low(exponent / lax.optimization_barrier(jnp.sum(exponent, axis=-1, keepdims=True)))
    attended = jnp.einsum('hqk,khd->qhd', attn_probs, values_act, precision=HIGHEST).reshape(SLOTS, D)
    attended = low(low_back(attended))
    residual = mixed_in + low_back(jnp.dot(attended, w_out, precision=HIGHEST))
    normed_two = low(layer_norm(residual, gain_two, shift_two))
    hidden_pre = low_back(jnp.dot(normed_two, w_up, precision=HIGHEST) + bias_up)
    hidden_act = low(gelu_tanh(hidden_pre))
    return residual + low_back(jnp.dot(hidden_act, w_down, precision=HIGHEST) + bias_down)

def row_forward(inputs, lengths, counts, params):
    loops_slot, allowed = row_layout(lengths, counts)
    current = inputs
    for loop_turn in range(LOOPS):
        renewed = block_forward(current, inputs, allowed, params)
        current = jnp.where((loops_slot > loop_turn)[:, None], renewed, current)
    return current

def reference(tokens, item_lengths, loop_counts, w_query, w_key, w_value, w_out, w_up, w_down, gain_one, shift_one, gain_two, shift_two, bias_up, bias_down, cotangent):
    weights = tuple((weight.astype(jnp.float32) for weight in (w_query, w_key, w_value, w_out, w_up, w_down, gain_one, shift_one, gain_two, shift_two, bias_up, bias_down)))

    def forward_all(inputs, params):

        def one_row(packed):
            return row_forward(packed[0], packed[1], packed[2], params)
        return lax.map(jax.checkpoint(one_row), (inputs, item_lengths, loop_counts))
    output, pullback = jax.vjp(forward_all, tokens.astype(jnp.float32), weights)
    input_grad, weight_grads = pullback(cotangent.astype(jnp.float32))
    return (output.astype(jnp.bfloat16), input_grad.astype(jnp.bfloat16), weight_grads[0], weight_grads[1], weight_grads[2], weight_grads[3], weight_grads[4], weight_grads[5], weight_grads[6], weight_grads[7], weight_grads[8], weight_grads[9], weight_grads[10], weight_grads[11])
```

```python
import functools
import math

import jax
import jax.numpy as jnp
from jax import lax
from jax.experimental import pallas as pl
from jax.experimental.pallas import tpu as pltpu
from jax.sharding import PartitionSpec as P

F32, BF = jnp.float32, jnp.bfloat16
MESH = pl.DeviceIdType.MESH
HEADS = 4
NORM_EPS = 1e-05
MASK_FILL = -1e30
C = 256
QB = 128
NN = (((1,), (0,)), ((), ()))
NT = (((1,), (1,)), ((), ()))
TN = (((0,), (0,)), ((), ()))
C0 = math.sqrt(2 / math.pi)
C1 = C0 * 0.044715

SMALL, WQ, WK, WV, WO, WU, WD = 0, 1, 2, 3, 4, 5, 10
SLABS = 14
GROUP_A, GROUP_B, GROUP_C = (0, 2), (4, 3), (10, 2)


def dot(a, b, dims=NN):
    return lax.dot_general(a, b, dims, preferred_element_type=F32)


class Exchange:
    def __init__(self, line, plane):
        self.line, self.plane = line, plane
        self.n = line * plane
        self.core = lax.axis_index("dp")
        self.me = lax.axis_index("wide")
        self.a = self.me // plane
        self.p = self.me % plane

    def chip(self, a, p):
        return {"dp": self.core, "wide": a * self.plane + p}

    def sibling(self):
        return {"dp": 1 - self.core, "wide": self.me}

    def along(self, step):
        return lax.rem(self.a + step, self.line)

    def across(self, step):
        return lax.rem(self.p + step, self.plane)


def send(src, dst, sems, k, device):
    copy = pltpu.make_async_remote_copy(
        src_ref=src,
        dst_ref=dst,
        send_sem=sems[0].at[k],
        recv_sem=sems[1].at[k],
        device_id=device,
        device_id_type=MESH,
    )
    copy.start()
    return copy


def arrived(copies):
    for copy in copies:
        copy.wait_recv()


def left(copies):
    for copy in copies:
        copy.wait_send()


def body(names, line, plane, r, *refs):
    s = dict(zip(names, refs))
    tok, cot, lens, cnts = s["tok"], s["cot"], s["lens"], s["cnts"]
    out, ing, res = s["out"], s["ing"], s["res"]
    wb, G, gs, small = s["wb"], s["G"], s["gs"], s["small"]
    gb = s.get("gb", wb)
    S, D = tok.shape
    nb = S // QB
    n = line * plane
    rp = wb.shape[3]
    x = Exchange(line, plane)
    core, me = x.core, x.me

    barrier = pltpu.get_barrier_semaphore()
    pl.semaphore_signal(barrier, inc=1, device_id=x.sibling(), device_id_type=MESH)
    for k in range(1, n):
        pl.semaphore_signal(
            barrier,
            inc=1,
            device_id={"dp": core, "wide": lax.rem(me + k, n)},
            device_id_type=MESH,
        )

    lanes = lax.broadcasted_iota(jnp.int32, (16, D), 1)
    rows16 = lax.broadcasted_iota(jnp.int32, (16, D), 0)
    tile = s["tile"]
    tile[...] = jnp.zeros((16, D), F32)
    for i, key in enumerate(("g1", "s1", "g2", "s2", "bd")):
        tile[i : i + 1, 0:r] = s[key][...].astype(F32)
    own = pltpu.roll(tile[...], me * r, axis=1)
    tile[0:1, 0 : 4 * r] = s["bu"][...].astype(F32)
    ups = jnp.broadcast_to(tile[0:1, :], (16, D))
    ups = jnp.where((lanes < 4 * r) & (rows16 == 5 + (me * 4 * r) // D), ups, 0.0)
    small_own = jnp.where(rows16 < 5, own, pltpu.roll(ups, lax.rem(me * 4 * r, D), axis=1)).astype(BF)
    first = jnp.where(core == 0, 1.0, 0.0).astype(BF)
    second = jnp.where(core == 0, 0.0, 1.0).astype(BF)

    def pad(v):
        return v if rp == r else jnp.concatenate([v.astype(F32), jnp.zeros((rp - r, D), F32)], axis=0).astype(BF)

    up = [pad(s["up"][:, c * D : (c + 1) * D]) for c in range(4)]
    down = [pad(s["down"][:, c * D : (c + 1) * D]) for c in range(4)]
    q_own, k_own, v_own, o_own = (pad(s[key][...]) for key in ("wq", "wk", "wv", "wo"))
    for (base, half), parts in (
        (GROUP_A, ((small_own, k_own), (q_own, v_own))),
        (GROUP_B, ((o_own, up[2]), (up[0], up[3]), (up[1], up[3]))),
        (GROUP_C, ((down[0], down[2]), (down[1], down[3]))),
    ):
        for i, (of_first, of_second) in enumerate(parts):
            wb[base + half * core + i, x.a, x.p] = of_first * first + of_second * second

    slot = lax.broadcasted_iota(jnp.int32, (nb, QB), 0) * QB + lax.broadcasted_iota(jnp.int32, (nb, QB), 1)
    end = jnp.int32(0)
    start_of = jnp.zeros((nb, QB), jnp.int32)
    loops_of = jnp.zeros((nb, QB), jnp.int32)
    for j in range(lens.shape[1]):
        inside = slot >= end
        start_of = jnp.where(inside, end, start_of)
        loops_of = jnp.where(inside, cnts[0, j], loops_of)
        end = end + lens[0, j]
    start_t = jnp.transpose(start_of.astype(F32))
    loops_t = jnp.transpose(loops_of.astype(F32))
    kk = lax.broadcasted_iota(jnp.int32, (QB, 2 * QB), 1).astype(F32)
    qq = lax.broadcasted_iota(jnp.int32, (QB, 2 * QB), 0).astype(F32)
    for b in range(nb):
        ok = (kk >= start_t[:, b : b + 1] - (b - 1) * QB) & (kk <= qq + QB)
        if b == 0:
            ok = ok & (kk >= QB)
        s["mask"][b] = jnp.where(ok, 0.0, MASK_FILL)
        s["act"][pl.ds(b * QB, QB), :] = jnp.broadcast_to(
            jnp.where(loops_t[:, b : b + 1] > 1, 1.0, 0.0), (QB, 128)
        )
    lane_head = lax.broadcasted_iota(jnp.int32, (1, D), 1) // (D // HEADS)
    hm = [jnp.where(lane_head == h, 1.0, 0.0).astype(BF) for h in range(HEADS)]
    for t in range(2):
        s["k"][t, 0:QB, :] = jnp.zeros((QB, D), BF)
        s["v"][t, 0:QB, :] = jnp.zeros((QB, D), BF)
    G[...] = jnp.zeros(G.shape, F32)
    gs[...] = jnp.zeros(gs.shape, F32)

    pl.semaphore_wait(barrier, n)

    def mine(group, buf=wb):
        base, half = group
        return buf.at[pl.ds(base + half * core, half)]

    sem = {key: (s["send_" + key], s["recv_" + key]) for key in SEMS(line, plane)}
    to_a = [
        send(mine(GROUP_A).at[:, x.a, x.p], mine(GROUP_A).at[:, x.a, x.p], sem["a"], k - 1,
             {"dp": core, "wide": lax.rem(me + k, n)})
        for k in range(1, n)
    ]
    to_b = [
        send(mine(GROUP_B).at[:, x.a, x.p], mine(GROUP_B).at[:, x.a, x.p], sem["b1"], k - 1,
             x.chip(x.along(k), x.p))
        for k in range(1, line)
    ]
    to_c = [
        send(mine(GROUP_C).at[:, x.a, x.p], mine(GROUP_C).at[:, x.a, x.p], sem["c1"], k - 1,
             x.chip(x.a, x.across(k)))
        for k in range(1, plane)
    ]
    arrived(to_a)
    share_a = [send(mine(GROUP_A), mine(GROUP_A), sem["sib"], 0, x.sibling())]
    arrived(to_b)
    to_b2 = [
        send(mine(GROUP_B).at[:, :, x.p], mine(GROUP_B).at[:, :, x.p], sem["b2"], k - 1,
             x.chip(x.a, x.across(k)))
        for k in range(1, plane)
    ]
    arrived(to_c)
    to_c2 = [
        send(mine(GROUP_C).at[:, x.a], mine(GROUP_C).at[:, x.a], sem["c2"], k - 1,
             x.chip(x.along(k), x.p))
        for k in range(1, line)
    ]
    arrived(share_a)
    whole_small = wb[SMALL].reshape(n, rp, D).astype(F32)
    small[...] = jnp.sum(whole_small, axis=0)[0:16]

    def W(i):
        return wb[i].reshape(D, D) if rp == r else s["wf"][i]

    def places():
        row = lax.broadcasted_iota(jnp.int32, (D, n * rp), 0)
        place = lax.broadcasted_iota(jnp.int32, (D, n * rp), 1)
        return jnp.where(place == (row // r) * rp + lax.rem(row, r), 1.0, 0.0).astype(BF)

    def unpack(base, count):
        if rp != r:

            @pl.loop(base, base + count)
            def _(i):
                s["wf"][i] = dot(places(), wb[i].reshape(n * rp, D)).astype(BF)

    def wide(v):
        return jnp.concatenate([v, v], axis=1)

    def norm_fwd(v, g, b):
        mean = jnp.mean(v, axis=1, keepdims=True)
        cen = v - mean
        var = jnp.mean(cen * cen, axis=1, keepdims=True)
        rstd = lax.rsqrt(var + NORM_EPS)
        z = cen * rstd
        return z, rstd, (z * g + b).astype(BF)

    def forward_attention(t, i):
        r0 = pl.multiple_of(i * C, C)
        rows = pl.ds(r0, C)
        tk = tok[rows, :].astype(F32)
        mixed = tk + tk if t == 0 else s["state"][rows, :] + tk
        z1, r1, n1 = norm_fwd(mixed, small[0:1, :], small[1:2, :])
        s["z1"][t, rows, :] = z1
        s["r1"][t, rows, :] = jnp.broadcast_to(r1, (C, 128))
        s["n1"][t, rows, :] = n1
        q = dot(n1, W(WQ)).astype(BF)
        s["q"][t, rows, :] = q
        s["k"][t, pl.ds(r0 + QB, C), :] = dot(n1, W(WK)).astype(BF)
        s["v"][t, pl.ds(r0 + QB, C), :] = dot(n1, W(WV)).astype(BF)
        for u in range(C // QB):
            b = i * (C // QB) + u
            win = pl.ds(pl.multiple_of(b * QB, QB), 2 * QB)
            kw, vw = s["k"][t, win, :], s["v"][t, win, :]
            qb = q[u * QB : (u + 1) * QB]
            qs = jnp.concatenate([qb * hm[h] for h in range(HEADS)], axis=0)
            sc = dot(qs, kw, NT)
            mask = s["mask"][b]
            ps = []
            for h in range(HEADS):
                e = sc[h * QB : (h + 1) * QB] * (D // HEADS) ** -0.5 + mask
                e = jnp.exp(e - jnp.max(e, axis=1, keepdims=True))
                ps.append((e * (1.0 / jnp.sum(e, axis=1, keepdims=True))).astype(BF))
            p = jnp.concatenate(ps, axis=0)
            s["p"][t, b] = p
            o = dot(p, vw)
            at = o[0:QB]
            for h in range(1, HEADS):
                at = jnp.where(lane_head == h, o[h * QB : (h + 1) * QB], at)
            s["at"][t, pl.ds(pl.multiple_of(b * QB, QB), QB), :] = at.astype(BF)
        s["mixed"][rows, :] = mixed

    def forward_hidden(t, i):
        rows = pl.ds(pl.multiple_of(i * C, C), C)
        resid = s["mixed"][rows, :] + dot(s["at"][t, rows, :], W(WO), NT)
        z2, r2, n2 = norm_fwd(resid, small[2:3, :], small[3:4, :])
        s["z2"][t, rows, :] = z2
        s["r2"][t, rows, :] = jnp.broadcast_to(r2, (C, 128))
        s["n2"][t, rows, :] = n2
        acc = resid + small[4:5, :]
        for c in range(4):
            hp = dot(n2, W(WU + c)) + small[5 + c : 6 + c, :]
            v2 = hp * hp
            th = jnp.tanh(hp * (C1 * v2 + C0))
            pr = 0.5 * th + 0.5
            g = hp * pr
            d = pr + g * (1.0 - pr) * ((6 * C1) * v2 + (2 * C0))
            g = g.astype(BF)
            s["h"][t, c, rows, :] = g
            s["d"][t, c, rows, :] = d.astype(BF)
            acc = acc + dot(g, W(WD + c), NT)
        if t == 0:
            s["state"][rows, :] = acc
        else:
            act = wide(s["act"][rows, :])
            out[rows, :] = jnp.where(act > 0, acc, s["state"][rows, :]).astype(BF)

    def norm_bwd(dn, g, z, rstd, gi):
        e = dn * g
        gs[gi : gi + 1, :] += jnp.sum(dn * z, axis=0, keepdims=True)
        gs[gi + 1 : gi + 2, :] += jnp.sum(dn, axis=0, keepdims=True)
        m1 = jnp.mean(e, axis=1, keepdims=True)
        m2 = jnp.mean(e * z, axis=1, keepdims=True)
        return wide(rstd) * (e - m1 - z * m2)

    def backward_hidden(t, i):
        rows = pl.ds(pl.multiple_of(i * C, C), C)
        if t == 1:
            br = jnp.where(wide(s["act"][rows, :]) > 0, cot[rows, :].astype(F32), 0.0)
        else:
            br = s["state"][rows, :]
        b2 = br.astype(BF)
        gs[4:5, :] += jnp.sum(br, axis=0, keepdims=True)
        b2t = b2.T
        n2t = s["n2"][t, rows, :].T
        dn2 = jnp.zeros((C, D), F32)
        for c in range(4):
            G[WD + c] += dot(b2t, s["h"][t, c, rows, :])
            dp = s["d"][t, c, rows, :].astype(F32) * dot(b2, W(WD + c))
            gs[5 + c : 6 + c, :] += jnp.sum(dp, axis=0, keepdims=True)
            dp = dp.astype(BF)
            G[WU + c] += dot(n2t, dp)
            dn2 = dn2 + dot(dp, W(WU + c), NT)
        bres = br + norm_bwd(dn2, small[2:3, :], s["z2"][t, rows, :], s["r2"][t, rows, :], 2)
        s["bres"][rows, :] = bres
        b1 = bres.astype(BF)
        G[WO] += dot(b1.T, s["at"][t, rows, :])
        s["do"][rows, :] = dot(b1, W(WO)).astype(BF)

    def backward_attention(t, i):
        r0 = pl.multiple_of(i * C, C)
        rows = pl.ds(r0, C)
        for u in reversed(range(C // QB)):
            b = i * (C // QB) + u
            win = pl.ds(pl.multiple_of(b * QB, QB), 2 * QB)
            qrows = pl.ds(pl.multiple_of(b * QB, QB), QB)
            kw, vw = s["k"][t, win, :], s["v"][t, win, :]
            qb, dob = s["q"][t, qrows, :], s["do"][qrows, :]
            qs = jnp.concatenate([qb * hm[h] for h in range(HEADS)], axis=0)
            dos = jnp.concatenate([dob * hm[h] for h in range(HEADS)], axis=0)
            p = s["p"][t, b]
            dp = dot(dos, vw, NT)
            pf = p.astype(F32)
            tt = pf * dp
            ds_ = (tt - pf * jnp.sum(tt, axis=1, keepdims=True)).astype(BF)
            dq = dot(ds_, kw)
            a = dq[0:QB]
            for h in range(1, HEADS):
                a = jnp.where(lane_head == h, dq[h * QB : (h + 1) * QB], a)
            s["dq"][pl.ds(u * QB, QB), :] = (a * (D // HEADS) ** -0.5).astype(BF)
            s["dv"][win, :] += dot(p, dos, TN)
            s["dk"][win, :] += dot(ds_, qs, TN)
        dq = s["dq"][...]
        own_keys = pl.ds(r0 + QB, C)
        dk = (s["dk"][own_keys, :] * (D // HEADS) ** -0.5).astype(BF)
        dv = s["dv"][own_keys, :].astype(BF)
        n1t = s["n1"][t, rows, :].T
        G[WQ] += dot(n1t, dq)
        G[WK] += dot(n1t, dk)
        G[WV] += dot(n1t, dv)
        dn1 = dot(dq, W(WQ), NT) + dot(dk, W(WK), NT) + dot(dv, W(WV), NT)
        bm = s["bres"][rows, :] + norm_bwd(dn1, small[0:1, :], s["z1"][t, rows, :], s["r1"][t, rows, :], 0)
        if t == 1:
            s["bi"][rows, :] = bm
            s["state"][rows, :] = jnp.where(wide(s["act"][rows, :]) > 0, 0.0, cot[rows, :].astype(F32)) + bm
        else:
            ing[rows, :] = (s["bi"][rows, :] + 2.0 * bm).astype(BF)

    chunks = S // C
    unpack(WQ, 3)

    @pl.loop(0, chunks)
    def _(i):
        forward_attention(0, i)

    arrived(to_b2)
    share_b = [send(mine(GROUP_B), mine(GROUP_B), sem["sib"], 1, x.sibling())]
    arrived(to_c2)
    share_c = [send(mine(GROUP_C), mine(GROUP_C), sem["sib"], 2, x.sibling())]
    arrived(share_b + share_c)
    unpack(WO, 5)
    unpack(WD, 4)

    @pl.loop(0, chunks)
    def _(i):
        forward_hidden(0, i)

    @pl.loop(0, chunks)
    def _(i):
        forward_attention(1, i)
        forward_hidden(1, i)

    s["dk"][...] = jnp.zeros(s["dk"].shape, F32)
    s["dv"][...] = jnp.zeros(s["dv"].shape, F32)

    @pl.loop(0, chunks)
    def _(i):
        backward_hidden(1, chunks - 1 - i)
        backward_attention(1, chunks - 1 - i)

    @pl.loop(0, chunks)
    def _(i):
        backward_hidden(0, chunks - 1 - i)

    def stage(base, count):
        @pl.loop(base, base + count)
        def _(i):
            if rp == r:
                gb[i] = G[i].astype(BF).reshape(line, plane, r, D)
            else:
                gb[i] = dot(places(), G[i].astype(BF), TN).astype(BF).reshape(line, plane, rp, D)

    def swap(group, inbox, k):
        base, half = group
        return [send(gb.at[pl.ds(base + half * (1 - core), half)], inbox, sem["rsib"], k, x.sibling())]

    def add_swapped(copies, group, inbox):
        arrived(copies)
        base, half = group
        @pl.loop(0, half)
        def _(i):
            at = base + half * core + i
            gb[at] = (gb[at].astype(F32) + inbox[i].astype(F32)).astype(BF)

    def finished(group, k, total):
        base, half = group
        for i in range(half):
            res[base + half * core + i] = total[i]
        part = res.at[pl.ds(base + half * core, half)]
        return [send(part, part, sem["fsib"], k, x.sibling())]

    left(to_a + to_b + to_c + to_b2 + to_c2 + share_a + share_b + share_c)
    stage(WO, 5)
    gb[WO + 5] = jnp.zeros(gb.shape[1:], BF)
    stage(WD, 4)
    swap_b = swap(GROUP_B, s["inb"], 1)
    swap_c = swap(GROUP_C, s["inc"], 2)

    s["dk"][...] = jnp.zeros(s["dk"].shape, F32)
    s["dv"][...] = jnp.zeros(s["dv"].shape, F32)
    backward_attention(0, chunks - 1)
    add_swapped(swap_b, GROUP_B, s["inb"])
    from_b = [
        send(mine(GROUP_B, gb).at[:, :, x.across(k)], s["inb1"].at[k - 1], sem["rb1"], k - 1,
             x.chip(x.a, x.across(k)))
        for k in range(1, plane)
    ]
    add_swapped(swap_c, GROUP_C, s["inc"])
    from_c = [
        send(mine(GROUP_C, gb).at[:, x.along(k)], s["inc1"].at[k - 1], sem["rc1"], k - 1,
             x.chip(x.along(k), x.p))
        for k in range(1, line)
    ]
    for i in range(chunks - 2, 0, -1):
        backward_attention(0, i)
    arrived(from_b)
    sum_b = mine(GROUP_B, gb)[:, :, x.p].astype(F32)
    for k in range(1, plane):
        sum_b = sum_b + s["inb1"][k - 1].astype(F32)
    s["sumb"][...] = sum_b.astype(BF)
    from_b2 = [
        send(s["sumb"].at[:, x.along(k)], s["inb2"].at[k - 1], sem["rb2"], k - 1, x.chip(x.along(k), x.p))
        for k in range(1, line)
    ]
    arrived(from_c)
    sum_c = mine(GROUP_C, gb)[:, x.a].astype(F32)
    for k in range(1, line):
        sum_c = sum_c + s["inc1"][k - 1].astype(F32)
    s["sumc"][...] = sum_c.astype(BF)
    from_c2 = [
        send(s["sumc"].at[:, x.across(k)], s["inc2"].at[k - 1], sem["rc2"], k - 1, x.chip(x.a, x.across(k)))
        for k in range(1, plane)
    ]
    backward_attention(0, 0)
    stage(WQ, 3)
    gb[SMALL] = jnp.broadcast_to(gs[...].astype(BF)[None, None], (line, plane, 16, D))
    swap_a = swap(GROUP_A, s["ina"], 0)
    arrived(from_b2)
    total = s["sumb"][:, x.a].astype(F32)
    for k in range(1, line):
        total = total + s["inb2"][k - 1].astype(F32)
    done_b = finished(GROUP_B, 1, total)
    arrived(from_c2)
    total = s["sumc"][:, x.p].astype(F32)
    for k in range(1, plane):
        total = total + s["inc2"][k - 1].astype(F32)
    done_c = finished(GROUP_C, 2, total)
    add_swapped(swap_a, GROUP_A, s["ina"])
    from_a = []
    for k in range(1, n):
        to = lax.rem(me + k, n)
        from_a.append(
            send(mine(GROUP_A, gb).at[:, to // plane, lax.rem(to, plane)], s["ina1"].at[k - 1], sem["ra"], k - 1,
                 {"dp": core, "wide": to})
        )
    arrived(from_a)
    total = mine(GROUP_A, gb)[:, x.a, x.p].astype(F32)
    for k in range(1, n):
        total = total + s["ina1"][k - 1].astype(F32)
    done_a = finished(GROUP_A, 0, total)
    arrived(done_a + done_b + done_c)
    left(swap_a + swap_b + swap_c + from_a + from_b + from_b2 + from_c + from_c2)
    left(done_a + done_b + done_c)


def SEMS(line, plane):
    n = line * plane
    return {
        "a": n - 1, "b1": line - 1, "c1": plane - 1, "b2": plane - 1, "c2": line - 1, "sib": 3,
        "rsib": 3, "rb1": plane - 1, "rb2": line - 1, "rc1": line - 1, "rc2": plane - 1, "ra": n - 1, "fsib": 3,
    }


def scratch(S, D, line, plane, rp):
    nb, n = S // QB, line * plane
    V = pltpu.VMEM
    shapes = dict(
        tile=V((16, D), F32), small=V((16, D), F32),
        wb=V((SLABS, line, plane, rp, D), BF),
        G=V((SLABS, D, D), F32), gs=V((16, D), F32),
        ina=V((2, line, plane, rp, D), BF), inb=V((3, line, plane, rp, D), BF), inc=V((2, line, plane, rp, D), BF),
        ina1=V((n - 1, 2, rp, D), BF),
        inb1=V((plane - 1, 3, line, rp, D), BF), inb2=V((line - 1, 3, rp, D), BF), sumb=V((3, line, rp, D), BF),
        inc1=V((line - 1, 2, plane, rp, D), BF), inc2=V((plane - 1, 2, rp, D), BF), sumc=V((2, plane, rp, D), BF),
        mask=V((nb, QB, 2 * QB), F32), act=V((S, 128), F32), state=V((S, D), F32), mixed=V((S, D), F32),
        z1=V((2, S, D), F32), r1=V((2, S, 128), F32), n1=V((2, S, D), BF),
        z2=V((2, S, D), F32), r2=V((2, S, 128), F32), n2=V((2, S, D), BF),
        q=V((2, S, D), BF), k=V((2, S + QB, D), BF), v=V((2, S + QB, D), BF),
        p=V((2, nb, HEADS * QB, 2 * QB), BF), at=V((2, S, D), BF),
        h=V((2, 4, S, D), BF), d=V((2, 4, S, D), BF),
        bres=V((S, D), F32), do=V((S, D), BF),
        dq=V((C, D), BF), dk=V((S + QB, D), F32), dv=V((S + QB, D), F32), bi=V((S, D), F32),
    )
    if D // n != rp:
        shapes["wf"] = V((SLABS, D, D), BF)
    else:
        shapes["gb"] = V((SLABS, line, plane, rp, D), BF)
    for key, count in SEMS(line, plane).items():
        shapes["send_" + key] = pltpu.SemaphoreType.DMA((count,))
        shapes["recv_" + key] = pltpu.SemaphoreType.DMA((count,))
    return shapes


def finish(r, *refs):
    out_in, ing_in, res, out, ing, gq, gk, gv, go, gu, gd, gg1, gs1, gg2, gs2, gbu, gbd, sems = refs
    copies = [pltpu.make_async_copy(out_in, out, sems.at[0]), pltpu.make_async_copy(ing_in, ing, sems.at[1])]
    for copy in copies:
        copy.start()
    D = res.shape[2]
    me = lax.axis_index("wide")
    for ref, at in ((gq, WQ), (gk, WK), (gv, WV), (go, WO)):
        ref[...] = res[at, 0:r, :]
    for c in range(4):
        gu[:, c * D : (c + 1) * D] = res[WU + c, 0:r, :]
        gd[:, c * D : (c + 1) * D] = res[WD + c, 0:r, :]
    tile = res[SMALL, 0:16, :]
    own = pltpu.roll(tile, lax.rem(D - me * r, D), axis=1)
    for i, ref in enumerate((gg1, gs1, gg2, gs2, gbd)):
        ref[...] = own[i : i + 1, 0:r]
    row = jnp.zeros((1, D), F32)
    for c in range(4):
        row = jnp.where((me * 4 * r) // D == c, tile[5 + c : 6 + c, :], row)
    row = jnp.broadcast_to(row, (8, D))
    gbu[...] = pltpu.roll(row, lax.rem(D - lax.rem(me * 4 * r, D), D), axis=1)[0:1, 0 : 4 * r]
    for copy in copies:
        copy.wait()


def on_device(sizes, *args):
    (tokens, lengths, counts, wq, wk, wv, wo, wu, wd, g1, s1, g2, s2, bu, bd, cot) = args
    line, plane = sizes
    S, D = tokens.shape[1:]
    r = wq.shape[0]
    rp = max(r, 16)
    vm = pl.BlockSpec(memory_space=pltpu.VMEM)
    sm = pl.BlockSpec(memory_space=pltpu.SMEM)
    hbm = pl.BlockSpec(memory_space=pl.ANY)
    inputs = dict(
        tok=tokens[0], cot=cot[0], lens=lengths, cnts=counts, wq=wq, wk=wk, wv=wv, wo=wo.T, up=wu, down=wd.T,
        g1=g1[None], s1=s1[None], g2=g2[None], s2=s2[None], bu=bu[None], bd=bd[None],
    )
    shapes = scratch(S, D, line, plane, rp)
    names = [*inputs, "out", "ing", "res", *shapes]
    out, ing, res = pl.pallas_call(
        functools.partial(body, names, line, plane, r),
        out_shape=(
            jax.ShapeDtypeStruct((S, D), BF),
            jax.ShapeDtypeStruct((S, D), BF),
            jax.ShapeDtypeStruct((SLABS, rp, D), F32),
        ),
        in_specs=[sm if key in ("lens", "cnts") else vm for key in inputs],
        out_specs=(vm, vm, vm),
        scratch_shapes=list(shapes.values()),
        compiler_params=pltpu.CompilerParams(
            collective_id=0, has_side_effects=True, vmem_limit_bytes=60 * 2**20
        ),
        name="loop_block",
    )(*inputs.values())
    f = lambda *shape: jax.ShapeDtypeStruct(shape, F32)
    out, ing, gq, gk, gv, go, gu, gd, gg1, gs1, gg2, gs2, gbu, gbd = pl.pallas_call(
        functools.partial(finish, r),
        out_shape=(
            jax.ShapeDtypeStruct((S, D), BF), jax.ShapeDtypeStruct((S, D), BF),
            f(r, D), f(r, D), f(r, D), f(r, D), f(r, 4 * D), f(r, 4 * D),
            f(1, r), f(1, r), f(1, r), f(1, r), f(1, 4 * r), f(1, r),
        ),
        in_specs=[hbm, hbm, vm],
        out_specs=(hbm, hbm) + (vm,) * 12,
        scratch_shapes=[pltpu.SemaphoreType.DMA((2,))],
        name="finish",
    )(out, ing, res)
    return (out[None], ing[None], gq, gk, gv, go.T, gu, gd.T, gg1[0], gs1[0], gg2[0], gs2[0], gbu[0], gbd[0])


def solution(mesh):
    wide = mesh.shape["wide"]
    line = 4 if wide % 4 == 0 else 1
    rows = P(("dp", "wide"), None, None)
    row = P(("dp", "wide"), None)
    first, second, one = P("wide", None), P(None, "wide"), P("wide")
    weights = (first, first, first, second, first, second)
    return jax.shard_map(
        functools.partial(on_device, (line, wide // line)),
        mesh=mesh,
        in_specs=(rows, row, row, *weights, *(one,) * 6, rows),
        out_specs=(rows, rows, *weights, *(one,) * 6),
        check_vma=False,
    )
```

```python
import functools
import math

import jax
import jax.numpy as jnp
from jax import lax
from jax.experimental import pallas as pl
from jax.experimental.pallas import tpu as pltpu
from jax.sharding import PartitionSpec as P

F32, BF = jnp.float32, jnp.bfloat16
MESH = pl.DeviceIdType.MESH
HEADS = 4
NORM_EPS = 1e-05
MASK_FILL = -1e30
C = 256
QB = 128
NN = (((1,), (0,)), ((), ()))
NT = (((1,), (1,)), ((), ()))
TN = (((0,), (0,)), ((), ()))
C0 = math.sqrt(2 / math.pi)
C1 = C0 * 0.044715

SMALL, WQ, WK, WV, WO, WU, WD = 0, 1, 2, 3, 4, 5, 10
SLABS = 14
GROUP_A, GROUP_B, GROUP_C = (0, 2), (4, 3), (10, 2)


def dot(a, b, dims=NN):
    return lax.dot_general(a, b, dims, preferred_element_type=F32)


class Exchange:
    def __init__(self, line, plane):
        self.line, self.plane = line, plane
        self.n = line * plane
        self.core = lax.axis_index("dp")
        self.me = lax.axis_index("wide")
        self.a = self.me // plane
        self.p = self.me % plane

    def chip(self, a, p):
        return {"dp": self.core, "wide": a * self.plane + p}

    def sibling(self):
        return {"dp": 1 - self.core, "wide": self.me}

    def along(self, step):
        return lax.rem(self.a + step, self.line)

    def across(self, step):
        return lax.rem(self.p + step, self.plane)


def send(src, dst, sems, k, device):
    copy = pltpu.make_async_remote_copy(
        src_ref=src,
        dst_ref=dst,
        send_sem=sems[0].at[k],
        recv_sem=sems[1].at[k],
        device_id=device,
        device_id_type=MESH,
    )
    copy.start()
    return copy


def arrived(copies):
    for copy in copies:
        copy.wait_recv()


def left(copies):
    for copy in copies:
        copy.wait_send()


def body(names, line, plane, r, *refs):
    s = dict(zip(names, refs))
    tok, cot, lens, cnts = s["tok"], s["cot"], s["lens"], s["cnts"]
    out, ing, res = s["out"], s["ing"], s["res"]
    wb, G, gs, small = s["wb"], s["G"], s["gs"], s["small"]
    gb = s.get("gb", wb)
    S, D = tok.shape
    nb = S // QB
    n = line * plane
    rp = wb.shape[3]
    x = Exchange(line, plane)
    core, me = x.core, x.me

    barrier = pltpu.get_barrier_semaphore()
    pl.semaphore_signal(barrier, inc=1, device_id=x.sibling(), device_id_type=MESH)
    for k in range(1, n):
        pl.semaphore_signal(
            barrier,
            inc=1,
            device_id={"dp": core, "wide": lax.rem(me + k, n)},
            device_id_type=MESH,
        )

    lanes = lax.broadcasted_iota(jnp.int32, (16, D), 1)
    rows16 = lax.broadcasted_iota(jnp.int32, (16, D), 0)
    tile = s["tile"]
    tile[...] = jnp.zeros((16, D), F32)
    for i, key in enumerate(("g1", "s1", "g2", "s2", "bd")):
        tile[i : i + 1, 0:r] = s[key][...].astype(F32)
    own = pltpu.roll(tile[...], me * r, axis=1)
    tile[0:1, 0 : 4 * r] = s["bu"][...].astype(F32)
    ups = jnp.broadcast_to(tile[0:1, :], (16, D))
    ups = jnp.where((lanes < 4 * r) & (rows16 == 5 + (me * 4 * r) // D), ups, 0.0)
    small_own = jnp.where(rows16 < 5, own, pltpu.roll(ups, lax.rem(me * 4 * r, D), axis=1)).astype(BF)
    first = jnp.where(core == 0, 1.0, 0.0).astype(BF)
    second = jnp.where(core == 0, 0.0, 1.0).astype(BF)

    def pad(v):
        return v if rp == r else jnp.concatenate([v.astype(F32), jnp.zeros((rp - r, D), F32)], axis=0).astype(BF)

    up = [pad(s["up"][:, c * D : (c + 1) * D]) for c in range(4)]
    down = [pad(s["down"][:, c * D : (c + 1) * D]) for c in range(4)]
    q_own, k_own, v_own, o_own = (pad(s[key][...]) for key in ("wq", "wk", "wv", "wo"))
    for (base, half), parts in (
        (GROUP_A, ((small_own, k_own), (q_own, v_own))),
        (GROUP_B, ((o_own, up[2]), (up[0], up[3]), (up[1], up[3]))),
        (GROUP_C, ((down[0], down[2]), (down[1], down[3]))),
    ):
        for i, (of_first, of_second) in enumerate(parts):
            wb[base + half * core + i, x.a, x.p] = of_first * first + of_second * second

    slot = lax.broadcasted_iota(jnp.int32, (nb, QB), 0) * QB + lax.broadcasted_iota(jnp.int32, (nb, QB), 1)
    end = jnp.int32(0)
    start_of = jnp.zeros((nb, QB), jnp.int32)
    loops_of = jnp.zeros((nb, QB), jnp.int32)
    for j in range(lens.shape[1]):
        inside = slot >= end
        start_of = jnp.where(inside, end, start_of)
        loops_of = jnp.where(inside, cnts[0, j], loops_of)
        end = end + lens[0, j]
    start_t = jnp.transpose(start_of.astype(F32))
    loops_t = jnp.transpose(loops_of.astype(F32))
    kk = lax.broadcasted_iota(jnp.int32, (QB, 2 * QB), 1).astype(F32)
    qq = lax.broadcasted_iota(jnp.int32, (QB, 2 * QB), 0).astype(F32)
    for b in range(nb):
        ok = (kk >= start_t[:, b : b + 1] - (b - 1) * QB) & (kk <= qq + QB)
        if b == 0:
            ok = ok & (kk >= QB)
        s["mask"][b] = jnp.where(ok, 0.0, MASK_FILL)
        s["act"][pl.ds(b * QB, QB), :] = jnp.broadcast_to(
            jnp.where(loops_t[:, b : b + 1] > 1, 1.0, 0.0), (QB, 128)
        )
    lane_head = lax.broadcasted_iota(jnp.int32, (1, D), 1) // (D // HEADS)
    hm = [jnp.where(lane_head == h, 1.0, 0.0).astype(BF) for h in range(HEADS)]
    for t in range(2):
        s["k"][t, 0:QB, :] = jnp.zeros((QB, D), BF)
        s["v"][t, 0:QB, :] = jnp.zeros((QB, D), BF)
    G[...] = jnp.zeros(G.shape, F32)
    gs[...] = jnp.zeros(gs.shape, F32)

    pl.semaphore_wait(barrier, n)

    def mine(group, buf=wb):
        base, half = group
        return buf.at[pl.ds(base + half * core, half)]

    sem = {key: (s["send_" + key], s["recv_" + key]) for key in SEMS(line, plane)}
    to_a = [
        send(mine(GROUP_A).at[:, x.a, x.p], mine(GROUP_A).at[:, x.a, x.p], sem["a"], k - 1,
             {"dp": core, "wide": lax.rem(me + k, n)})
        for k in range(1, n)
    ]
    to_b = [
        send(mine(GROUP_B).at[:, x.a, x.p], mine(GROUP_B).at[:, x.a, x.p], sem["b1"], k - 1,
             x.chip(x.along(k), x.p))
        for k in range(1, line)
    ]
    to_c = [
        send(mine(GROUP_C).at[:, x.a, x.p], mine(GROUP_C).at[:, x.a, x.p], sem["c1"], k - 1,
             x.chip(x.a, x.across(k)))
        for k in range(1, plane)
    ]
    arrived(to_a)
    share_a = [send(mine(GROUP_A), mine(GROUP_A), sem["sib"], 0, x.sibling())]
    arrived(to_b)
    to_b2 = [
        send(mine(GROUP_B).at[:, :, x.p], mine(GROUP_B).at[:, :, x.p], sem["b2"], k - 1,
             x.chip(x.a, x.across(k)))
        for k in range(1, plane)
    ]
    arrived(to_c)
    to_c2 = [
        send(mine(GROUP_C).at[:, x.a], mine(GROUP_C).at[:, x.a], sem["c2"], k - 1,
             x.chip(x.along(k), x.p))
        for k in range(1, line)
    ]
    arrived(share_a)
    whole_small = wb[SMALL].reshape(n, rp, D).astype(F32)
    small[...] = jnp.sum(whole_small, axis=0)[0:16]

    def W(i):
        return wb[i].reshape(D, D) if rp == r else s["wf"][i]

    def places():
        row = lax.broadcasted_iota(jnp.int32, (D, n * rp), 0)
        place = lax.broadcasted_iota(jnp.int32, (D, n * rp), 1)
        return jnp.where(place == (row // r) * rp + lax.rem(row, r), 1.0, 0.0).astype(BF)

    def unpack(base, count):
        if rp != r:

            @pl.loop(base, base + count)
            def _(i):
                s["wf"][i] = dot(places(), wb[i].reshape(n * rp, D)).astype(BF)

    def wide(v):
        return jnp.concatenate([v, v], axis=1)

    def norm_fwd(v, g, b):
        mean = jnp.mean(v, axis=1, keepdims=True)
        cen = v - mean
        var = jnp.mean(cen * cen, axis=1, keepdims=True)
        rstd = lax.rsqrt(var + NORM_EPS)
        z = cen * rstd
        return z, rstd, (z * g + b).astype(BF)

    def forward_attention(t, i):
        r0 = pl.multiple_of(i * C, C)
        rows = pl.ds(r0, C)
        tk = tok[rows, :].astype(F32)
        mixed = tk + tk if t == 0 else s["state"][rows, :] + tk
        z1, r1, n1 = norm_fwd(mixed, small[0:1, :], small[1:2, :])
        s["z1"][t, rows, :] = z1
        s["r1"][t, rows, :] = jnp.broadcast_to(r1, (C, 128))
        s["n1"][t, rows, :] = n1
        q = dot(n1, W(WQ)).astype(BF)
        s["q"][t, rows, :] = q
        s["k"][t, pl.ds(r0 + QB, C), :] = dot(n1, W(WK)).astype(BF)
        s["v"][t, pl.ds(r0 + QB, C), :] = dot(n1, W(WV)).astype(BF)
        for u in range(C // QB):
            b = i * (C // QB) + u
            win = pl.ds(pl.multiple_of(b * QB, QB), 2 * QB)
            kw, vw = s["k"][t, win, :], s["v"][t, win, :]
            qb = q[u * QB : (u + 1) * QB]
            qs = jnp.concatenate([qb * hm[h] for h in range(HEADS)], axis=0)
            sc = dot(qs, kw, NT)
            mask = s["mask"][b]
            ps = []
            for h in range(HEADS):
                e = sc[h * QB : (h + 1) * QB] * (D // HEADS) ** -0.5 + mask
                e = jnp.exp(e - jnp.max(e, axis=1, keepdims=True))
                ps.append((e * (1.0 / jnp.sum(e, axis=1, keepdims=True))).astype(BF))
            p = jnp.concatenate(ps, axis=0)
            s["p"][t, b] = p
            o = dot(p, vw)
            at = o[0:QB]
            for h in range(1, HEADS):
                at = jnp.where(lane_head == h, o[h * QB : (h + 1) * QB], at)
            s["at"][t, pl.ds(pl.multiple_of(b * QB, QB), QB), :] = at.astype(BF)
        s["mixed"][rows, :] = mixed

    def forward_hidden(t, i):
        rows = pl.ds(pl.multiple_of(i * C, C), C)
        resid = s["mixed"][rows, :] + dot(s["at"][t, rows, :], W(WO), NT)
        z2, r2, n2 = norm_fwd(resid, small[2:3, :], small[3:4, :])
        s["z2"][t, rows, :] = z2
        s["r2"][t, rows, :] = jnp.broadcast_to(r2, (C, 128))
        s["n2"][t, rows, :] = n2
        acc = resid + small[4:5, :]
        for c in range(4):
            hp = dot(n2, W(WU + c)) + small[5 + c : 6 + c, :]
            v2 = hp * hp
            th = jnp.tanh(hp * (C1 * v2 + C0))
            pr = 0.5 * th + 0.5
            g = hp * pr
            d = pr + g * (1.0 - pr) * ((6 * C1) * v2 + (2 * C0))
            g = g.astype(BF)
            s["h"][t, c, rows, :] = g
            s["d"][t, c, rows, :] = d.astype(BF)
            acc = acc + dot(g, W(WD + c), NT)
        if t == 0:
            s["state"][rows, :] = acc
        else:
            act = wide(s["act"][rows, :])
            out[rows, :] = jnp.where(act > 0, acc, s["state"][rows, :]).astype(BF)

    def norm_bwd(dn, g, z, rstd, gi):
        e = dn * g
        gs[gi : gi + 1, :] += jnp.sum(dn * z, axis=0, keepdims=True)
        gs[gi + 1 : gi + 2, :] += jnp.sum(dn, axis=0, keepdims=True)
        m1 = jnp.mean(e, axis=1, keepdims=True)
        m2 = jnp.mean(e * z, axis=1, keepdims=True)
        return wide(rstd) * (e - m1 - z * m2)

    def backward_hidden(t, i):
        rows = pl.ds(pl.multiple_of(i * C, C), C)
        if t == 1:
            br = jnp.where(wide(s["act"][rows, :]) > 0, cot[rows, :].astype(F32), 0.0)
        else:
            br = s["state"][rows, :]
        b2 = br.astype(BF)
        gs[4:5, :] += jnp.sum(br, axis=0, keepdims=True)
        b2t = b2.T
        n2t = s["n2"][t, rows, :].T
        dn2 = jnp.zeros((C, D), F32)
        for c in range(4):
            G[WD + c] += dot(b2t, s["h"][t, c, rows, :])
            dp = s["d"][t, c, rows, :].astype(F32) * dot(b2, W(WD + c))
            gs[5 + c : 6 + c, :] += jnp.sum(dp, axis=0, keepdims=True)
            dp = dp.astype(BF)
            G[WU + c] += dot(n2t, dp)
            dn2 = dn2 + dot(dp, W(WU + c), NT)
        bres = br + norm_bwd(dn2, small[2:3, :], s["z2"][t, rows, :], s["r2"][t, rows, :], 2)
        s["bres"][rows, :] = bres
        b1 = bres.astype(BF)
        G[WO] += dot(b1.T, s["at"][t, rows, :])
        s["do"][rows, :] = dot(b1, W(WO)).astype(BF)

    def backward_attention(t, i):
        r0 = pl.multiple_of(i * C, C)
        rows = pl.ds(r0, C)
        for u in reversed(range(C // QB)):
            b = i * (C // QB) + u
            win = pl.ds(pl.multiple_of(b * QB, QB), 2 * QB)
            qrows = pl.ds(pl.multiple_of(b * QB, QB), QB)
            kw, vw = s["k"][t, win, :], s["v"][t, win, :]
            qb, dob = s["q"][t, qrows, :], s["do"][qrows, :]
            qs = jnp.concatenate([qb * hm[h] for h in range(HEADS)], axis=0)
            dos = jnp.concatenate([dob * hm[h] for h in range(HEADS)], axis=0)
            p = s["p"][t, b]
            dp = dot(dos, vw, NT)
            pf = p.astype(F32)
            tt = pf * dp
            ds_ = (tt - pf * jnp.sum(tt, axis=1, keepdims=True)).astype(BF)
            dq = dot(ds_, kw)
            a = dq[0:QB]
            for h in range(1, HEADS):
                a = jnp.where(lane_head == h, dq[h * QB : (h + 1) * QB], a)
            s["dq"][pl.ds(u * QB, QB), :] = (a * (D // HEADS) ** -0.5).astype(BF)
            s["dv"][win, :] += dot(p, dos, TN)
            s["dk"][win, :] += dot(ds_, qs, TN)
        dq = s["dq"][...]
        own_keys = pl.ds(r0 + QB, C)
        dk = (s["dk"][own_keys, :] * (D // HEADS) ** -0.5).astype(BF)
        dv = s["dv"][own_keys, :].astype(BF)
        n1t = s["n1"][t, rows, :].T
        G[WQ] += dot(n1t, dq)
        G[WK] += dot(n1t, dk)
        G[WV] += dot(n1t, dv)
        dn1 = dot(dq, W(WQ), NT) + dot(dk, W(WK), NT) + dot(dv, W(WV), NT)
        bm = s["bres"][rows, :] + norm_bwd(dn1, small[0:1, :], s["z1"][t, rows, :], s["r1"][t, rows, :], 0)
        if t == 1:
            s["bi"][rows, :] = bm
            s["state"][rows, :] = jnp.where(wide(s["act"][rows, :]) > 0, 0.0, cot[rows, :].astype(F32)) + bm
        else:
            ing[rows, :] = (s["bi"][rows, :] + 2.0 * bm).astype(BF)

    chunks = S // C
    unpack(WQ, 3)

    @pl.loop(0, chunks)
    def _(i):
        forward_attention(0, i)

    arrived(to_b2)
    share_b = [send(mine(GROUP_B), mine(GROUP_B), sem["sib"], 1, x.sibling())]
    arrived(to_c2)
    share_c = [send(mine(GROUP_C), mine(GROUP_C), sem["sib"], 2, x.sibling())]
    arrived(share_b + share_c)
    unpack(WO, 5)
    unpack(WD, 4)

    @pl.loop(0, chunks)
    def _(i):
        forward_hidden(0, i)

    @pl.loop(0, chunks)
    def _(i):
        forward_attention(1, i)
        forward_hidden(1, i)

    s["dk"][...] = jnp.zeros(s["dk"].shape, F32)
    s["dv"][...] = jnp.zeros(s["dv"].shape, F32)

    @pl.loop(0, chunks)
    def _(i):
        backward_hidden(1, chunks - 1 - i)
        backward_attention(1, chunks - 1 - i)

    @pl.loop(0, chunks)
    def _(i):
        backward_hidden(0, chunks - 1 - i)

    def stage(base, count):
        @pl.loop(base, base + count)
        def _(i):
            if rp == r:
                gb[i] = G[i].astype(BF).reshape(line, plane, r, D)
            else:
                gb[i] = dot(places(), G[i].astype(BF), TN).astype(BF).reshape(line, plane, rp, D)

    def swap(group, inbox, k):
        base, half = group
        return [send(gb.at[pl.ds(base + half * (1 - core), half)], inbox, sem["rsib"], k, x.sibling())]

    def add_swapped(copies, group, inbox):
        arrived(copies)
        base, half = group
        @pl.loop(0, half)
        def _(i):
            at = base + half * core + i
            gb[at] = (gb[at].astype(F32) + inbox[i].astype(F32)).astype(BF)

    def finished(group, k, total):
        base, half = group
        for i in range(half):
            res[base + half * core + i] = total[i]
        part = res.at[pl.ds(base + half * core, half)]
        return [send(part, part, sem["fsib"], k, x.sibling())]

    left(to_a + to_b + to_c + to_b2 + to_c2 + share_a + share_b + share_c)
    stage(WO, 5)
    gb[WO + 5] = jnp.zeros(gb.shape[1:], BF)
    stage(WD, 4)
    swap_b = swap(GROUP_B, s["inb"], 1)
    swap_c = swap(GROUP_C, s["inc"], 2)

    s["dk"][...] = jnp.zeros(s["dk"].shape, F32)
    s["dv"][...] = jnp.zeros(s["dv"].shape, F32)
    backward_attention(0, chunks - 1)
    add_swapped(swap_b, GROUP_B, s["inb"])
    from_b = [
        send(mine(GROUP_B, gb).at[:, :, x.across(k)], s["inb1"].at[k - 1], sem["rb1"], k - 1,
             x.chip(x.a, x.across(k)))
        for k in range(1, plane)
    ]
    add_swapped(swap_c, GROUP_C, s["inc"])
    from_c = [
        send(mine(GROUP_C, gb).at[:, x.along(k)], s["inc1"].at[k - 1], sem["rc1"], k - 1,
             x.chip(x.along(k), x.p))
        for k in range(1, line)
    ]
    for i in range(chunks - 2, 0, -1):
        backward_attention(0, i)
    arrived(from_b)
    sum_b = mine(GROUP_B, gb)[:, :, x.p].astype(F32)
    for k in range(1, plane):
        sum_b = sum_b + s["inb1"][k - 1].astype(F32)
    s["sumb"][...] = sum_b.astype(BF)
    from_b2 = [
        send(s["sumb"].at[:, x.along(k)], s["inb2"].at[k - 1], sem["rb2"], k - 1, x.chip(x.along(k), x.p))
        for k in range(1, line)
    ]
    arrived(from_c)
    sum_c = mine(GROUP_C, gb)[:, x.a].astype(F32)
    for k in range(1, line):
        sum_c = sum_c + s["inc1"][k - 1].astype(F32)
    s["sumc"][...] = sum_c.astype(BF)
    from_c2 = [
        send(s["sumc"].at[:, x.across(k)], s["inc2"].at[k - 1], sem["rc2"], k - 1, x.chip(x.a, x.across(k)))
        for k in range(1, plane)
    ]
    backward_attention(0, 0)
    stage(WQ, 3)
    gb[SMALL] = jnp.broadcast_to(gs[...].astype(BF)[None, None], (line, plane, 16, D))
    swap_a = swap(GROUP_A, s["ina"], 0)
    arrived(from_b2)
    total = s["sumb"][:, x.a].astype(F32)
    for k in range(1, line):
        total = total + s["inb2"][k - 1].astype(F32)
    done_b = finished(GROUP_B, 1, total)
    arrived(from_c2)
    total = s["sumc"][:, x.p].astype(F32)
    for k in range(1, plane):
        total = total + s["inc2"][k - 1].astype(F32)
    done_c = finished(GROUP_C, 2, total)
    add_swapped(swap_a, GROUP_A, s["ina"])
    from_a = []
    for k in range(1, n):
        to = lax.rem(me + k, n)
        from_a.append(
            send(mine(GROUP_A, gb).at[:, to // plane, lax.rem(to, plane)], s["ina1"].at[k - 1], sem["ra"], k - 1,
                 {"dp": core, "wide": to})
        )
    arrived(from_a)
    total = mine(GROUP_A, gb)[:, x.a, x.p].astype(F32)
    for k in range(1, n):
        total = total + s["ina1"][k - 1].astype(F32)
    done_a = finished(GROUP_A, 0, total)
    arrived(done_a + done_b + done_c)
    left(swap_a + swap_b + swap_c + from_a + from_b + from_b2 + from_c + from_c2)
    left(done_a + done_b + done_c)


def SEMS(line, plane):
    n = line * plane
    return {
        "a": n - 1, "b1": line - 1, "c1": plane - 1, "b2": plane - 1, "c2": line - 1, "sib": 3,
        "rsib": 3, "rb1": plane - 1, "rb2": line - 1, "rc1": line - 1, "rc2": plane - 1, "ra": n - 1, "fsib": 3,
    }


def scratch(S, D, line, plane, rp):
    nb, n = S // QB, line * plane
    V = pltpu.VMEM
    shapes = dict(
        tile=V((16, D), F32), small=V((16, D), F32),
        wb=V((SLABS, line, plane, rp, D), BF),
        G=V((SLABS, D, D), F32), gs=V((16, D), F32),
        ina=V((2, line, plane, rp, D), BF), inb=V((3, line, plane, rp, D), BF), inc=V((2, line, plane, rp, D), BF),
        ina1=V((n - 1, 2, rp, D), BF),
        inb1=V((plane - 1, 3, line, rp, D), BF), inb2=V((line - 1, 3, rp, D), BF), sumb=V((3, line, rp, D), BF),
        inc1=V((line - 1, 2, plane, rp, D), BF), inc2=V((plane - 1, 2, rp, D), BF), sumc=V((2, plane, rp, D), BF),
        mask=V((nb, QB, 2 * QB), F32), act=V((S, 128), F32), state=V((S, D), F32), mixed=V((S, D), F32),
        z1=V((2, S, D), F32), r1=V((2, S, 128), F32), n1=V((2, S, D), BF),
        z2=V((2, S, D), F32), r2=V((2, S, 128), F32), n2=V((2, S, D), BF),
        q=V((2, S, D), BF), k=V((2, S + QB, D), BF), v=V((2, S + QB, D), BF),
        p=V((2, nb, HEADS * QB, 2 * QB), BF), at=V((2, S, D), BF),
        h=V((2, 4, S, D), BF), d=V((2, 4, S, D), BF),
        bres=V((S, D), F32), do=V((S, D), BF),
        dq=V((C, D), BF), dk=V((S + QB, D), F32), dv=V((S + QB, D), F32), bi=V((S, D), F32),
    )
    if D // n != rp:
        shapes["wf"] = V((SLABS, D, D), BF)
    else:
        shapes["gb"] = V((SLABS, line, plane, rp, D), BF)
    for key, count in SEMS(line, plane).items():
        shapes["send_" + key] = pltpu.SemaphoreType.DMA((count,))
        shapes["recv_" + key] = pltpu.SemaphoreType.DMA((count,))
    return shapes


def finish(r, *refs):
    out_in, ing_in, res, out, ing, gq, gk, gv, go, gu, gd, gg1, gs1, gg2, gs2, gbu, gbd = refs
    out[...] = out_in[...]
    ing[...] = ing_in[...]
    D = res.shape[2]
    me = lax.axis_index("wide")
    for ref, at in ((gq, WQ), (gk, WK), (gv, WV), (go, WO)):
        ref[...] = res[at, 0:r, :]
    for c in range(4):
        gu[:, c * D : (c + 1) * D] = res[WU + c, 0:r, :]
        gd[:, c * D : (c + 1) * D] = res[WD + c, 0:r, :]
    tile = res[SMALL, 0:16, :]
    own = pltpu.roll(tile, lax.rem(D - me * r, D), axis=1)
    for i, ref in enumerate((gg1, gs1, gg2, gs2, gbd)):
        ref[...] = own[i : i + 1, 0:r]
    row = jnp.zeros((1, D), F32)
    for c in range(4):
        row = jnp.where((me * 4 * r) // D == c, tile[5 + c : 6 + c, :], row)
    row = jnp.broadcast_to(row, (8, D))
    gbu[...] = pltpu.roll(row, lax.rem(D - lax.rem(me * 4 * r, D), D), axis=1)[0:1, 0 : 4 * r]


def on_device(sizes, *args):
    (tokens, lengths, counts, wq, wk, wv, wo, wu, wd, g1, s1, g2, s2, bu, bd, cot) = args
    line, plane = sizes
    S, D = tokens.shape[1:]
    r = wq.shape[0]
    rp = max(r, 16)
    vm = pl.BlockSpec(memory_space=pltpu.VMEM)
    sm = pl.BlockSpec(memory_space=pltpu.SMEM)
    inputs = dict(
        tok=tokens[0], cot=cot[0], lens=lengths, cnts=counts, wq=wq, wk=wk, wv=wv, wo=wo.T, up=wu, down=wd.T,
        g1=g1[None], s1=s1[None], g2=g2[None], s2=s2[None], bu=bu[None], bd=bd[None],
    )
    shapes = scratch(S, D, line, plane, rp)
    names = [*inputs, "out", "ing", "res", *shapes]
    out, ing, res = pl.pallas_call(
        functools.partial(body, names, line, plane, r),
        out_shape=(
            jax.ShapeDtypeStruct((S, D), BF),
            jax.ShapeDtypeStruct((S, D), BF),
            jax.ShapeDtypeStruct((SLABS, rp, D), F32),
        ),
        in_specs=[sm if key in ("lens", "cnts") else vm for key in inputs],
        out_specs=(vm, vm, vm),
        scratch_shapes=list(shapes.values()),
        compiler_params=pltpu.CompilerParams(
            collective_id=0, has_side_effects=True, vmem_limit_bytes=60 * 2**20
        ),
        name="loop_block",
    )(*inputs.values())
    f = lambda *shape: jax.ShapeDtypeStruct(shape, F32)
    out, ing, gq, gk, gv, go, gu, gd, gg1, gs1, gg2, gs2, gbu, gbd = pl.pallas_call(
        functools.partial(finish, r),
        out_shape=(
            jax.ShapeDtypeStruct((S, D), BF), jax.ShapeDtypeStruct((S, D), BF),
            f(r, D), f(r, D), f(r, D), f(r, D), f(r, 4 * D), f(r, 4 * D),
            f(1, r), f(1, r), f(1, r), f(1, r), f(1, 4 * r), f(1, r),
        ),
        in_specs=[vm] * 3,
        out_specs=(vm,) * 14,
        name="finish",
    )(out, ing, res)
    return (out[None], ing[None], gq, gk, gv, go.T, gu, gd.T, gg1[0], gs1[0], gg2[0], gs2[0], gbu[0], gbd[0])


def solution(mesh):
    wide = mesh.shape["wide"]
    line = 4 if wide % 4 == 0 else 1
    rows = P(("dp", "wide"), None, None)
    row = P(("dp", "wide"), None)
    first, second, one = P("wide", None), P(None, "wide"), P("wide")
    weights = (first, first, first, second, first, second)
    return jax.shard_map(
        functools.partial(on_device, (line, wide // line)),
        mesh=mesh,
        in_specs=(rows, row, row, *weights, *(one,) * 6, rows),
        out_specs=(rows, rows, *weights, *(one,) * 6),
        check_vma=False,
    )
```

```python
import functools
import math

import jax
import jax.numpy as jnp
from jax import lax
from jax.experimental import pallas as pl
from jax.experimental.pallas import tpu as pltpu
from jax.sharding import PartitionSpec as P

F32, BF = jnp.float32, jnp.bfloat16
MESH = pl.DeviceIdType.MESH
HEADS = 4
NORM_EPS = 1e-05
MASK_FILL = -1e30
QB = 128
NN = (((1,), (0,)), ((), ()))
NT = (((1,), (1,)), ((), ()))
TN = (((0,), (0,)), ((), ()))
C0 = math.sqrt(2 / math.pi)
C1 = C0 * 0.044715

SMALL, WQ, WK, WV, WO, WU, WD = 0, 1, 2, 3, 4, 5, 10
SLABS = 14
GROUP_A, GROUP_B, GROUP_C = (0, 2), (4, 3), (10, 2)


def dot(a, b, dims=NN):
    return lax.dot_general(a, b, dims, preferred_element_type=F32)


class Exchange:
    def __init__(self, line, plane):
        self.line, self.plane = line, plane
        self.n = line * plane
        self.core = lax.axis_index("dp")
        self.me = lax.axis_index("wide")
        self.a = self.me // plane
        self.p = self.me % plane

    def chip(self, a, p):
        return {"dp": self.core, "wide": a * self.plane + p}

    def sibling(self):
        return {"dp": 1 - self.core, "wide": self.me}

    def along(self, step):
        return lax.rem(self.a + step, self.line)

    def across(self, step):
        return lax.rem(self.p + step, self.plane)


def send(src, dst, sems, k, device):
    copy = pltpu.make_async_remote_copy(
        src_ref=src,
        dst_ref=dst,
        send_sem=sems[0].at[k],
        recv_sem=sems[1].at[k],
        device_id=device,
        device_id_type=MESH,
    )
    copy.start()
    return copy


def arrived(copies):
    for copy in copies:
        copy.wait_recv()


def left(copies):
    for copy in copies:
        copy.wait_send()


def layout(s):
    lens, cnts, G, gs = s["lens"], s["cnts"], s["G"], s["gs"]
    S, D = s["tok"].shape
    nb = S // QB
    slot = lax.broadcasted_iota(jnp.int32, (nb, QB), 0) * QB + lax.broadcasted_iota(jnp.int32, (nb, QB), 1)
    end = jnp.int32(0)
    start_of = jnp.zeros((nb, QB), jnp.int32)
    loops_of = jnp.zeros((nb, QB), jnp.int32)
    for j in range(lens.shape[1]):
        inside = slot >= end
        start_of = jnp.where(inside, end, start_of)
        loops_of = jnp.where(inside, cnts[0, j], loops_of)
        end = end + lens[0, j]
    start_t = jnp.transpose(start_of.astype(F32))
    loops_t = jnp.transpose(loops_of.astype(F32))
    kk = lax.broadcasted_iota(jnp.int32, (QB, 2 * QB), 1).astype(F32)
    qq = lax.broadcasted_iota(jnp.int32, (QB, 2 * QB), 0).astype(F32)
    for b in range(nb):
        ok = (kk >= start_t[:, b : b + 1] - (b - 1) * QB) & (kk <= qq + QB)
        if b == 0:
            ok = ok & (kk >= QB)
        s["mask"][b] = jnp.where(ok, 0.0, MASK_FILL)
        s["act"][pl.ds(b * QB, QB), :] = jnp.broadcast_to(
            jnp.where(loops_t[:, b : b + 1] > 1, 1.0, 0.0), (QB, 128)
        )
    for t in range(2):
        s["k"][t, 0:QB, :] = jnp.zeros((QB, D), BF)
        s["v"][t, 0:QB, :] = jnp.zeros((QB, D), BF)
    G[...] = jnp.zeros(G.shape, F32)
    gs[...] = jnp.zeros(gs.shape, F32)


def block(s, W, C):
    tok, cot, out, ing, small, G, gs = (s[key] for key in ("tok", "cot", "out", "ing", "small", "G", "gs"))
    D = tok.shape[1]
    lane_head = lax.broadcasted_iota(jnp.int32, (1, D), 1) // (D // HEADS)
    hm = [jnp.where(lane_head == h, 1.0, 0.0).astype(BF) for h in range(HEADS)]

    def wide(v):
        return jnp.concatenate([v, v], axis=1)

    def norm_fwd(v, g, b):
        mean = jnp.mean(v, axis=1, keepdims=True)
        cen = v - mean
        var = jnp.mean(cen * cen, axis=1, keepdims=True)
        rstd = lax.rsqrt(var + NORM_EPS)
        z = cen * rstd
        return z, rstd, (z * g + b).astype(BF)

    def forward_attention(t, i):
        r0 = pl.multiple_of(i * C, C)
        rows = pl.ds(r0, C)
        tk = tok[rows, :].astype(F32)
        mixed = tk + tk if t == 0 else s["state"][rows, :] + tk
        z1, r1, n1 = norm_fwd(mixed, small[0:1, :], small[1:2, :])
        s["z1"][t, rows, :] = z1
        s["r1"][t, rows, :] = jnp.broadcast_to(r1, (C, 128))
        s["n1"][t, rows, :] = n1
        q = dot(n1, W(WQ)).astype(BF)
        s["q"][t, rows, :] = q
        s["k"][t, pl.ds(r0 + QB, C), :] = dot(n1, W(WK)).astype(BF)
        s["v"][t, pl.ds(r0 + QB, C), :] = dot(n1, W(WV)).astype(BF)
        for u in range(C // QB):
            b = i * (C // QB) + u
            win = pl.ds(pl.multiple_of(b * QB, QB), 2 * QB)
            kw, vw = s["k"][t, win, :], s["v"][t, win, :]
            qb = q[u * QB : (u + 1) * QB]
            qs = jnp.concatenate([qb * hm[h] for h in range(HEADS)], axis=0)
            sc = dot(qs, kw, NT)
            mask = s["mask"][b]
            ps = []
            for h in range(HEADS):
                e = sc[h * QB : (h + 1) * QB] * (D // HEADS) ** -0.5 + mask
                e = jnp.exp(e - jnp.max(e, axis=1, keepdims=True))
                ps.append((e * (1.0 / jnp.sum(e, axis=1, keepdims=True))).astype(BF))
            p = jnp.concatenate(ps, axis=0)
            s["p"][t, b] = p
            o = dot(p, vw)
            at = o[0:QB]
            for h in range(1, HEADS):
                at = jnp.where(lane_head == h, o[h * QB : (h + 1) * QB], at)
            s["at"][t, pl.ds(pl.multiple_of(b * QB, QB), QB), :] = at.astype(BF)
        s["mixed"][rows, :] = mixed

    def forward_hidden(t, i):
        rows = pl.ds(pl.multiple_of(i * C, C), C)
        resid = s["mixed"][rows, :] + dot(s["at"][t, rows, :], W(WO), NT)
        z2, r2, n2 = norm_fwd(resid, small[2:3, :], small[3:4, :])
        s["z2"][t, rows, :] = z2
        s["r2"][t, rows, :] = jnp.broadcast_to(r2, (C, 128))
        s["n2"][t, rows, :] = n2
        acc = resid + small[4:5, :]
        for c in range(4):
            hp = dot(n2, W(WU + c)) + small[5 + c : 6 + c, :]
            v2 = hp * hp
            th = jnp.tanh(hp * (C1 * v2 + C0))
            pr = 0.5 * th + 0.5
            g = hp * pr
            d = pr + g * (1.0 - pr) * ((6 * C1) * v2 + (2 * C0))
            g = g.astype(BF)
            s["h"][t, c, rows, :] = g
            s["d"][t, c, rows, :] = d.astype(BF)
            acc = acc + dot(g, W(WD + c), NT)
        if t == 0:
            s["state"][rows, :] = acc
        else:
            act = wide(s["act"][rows, :])
            out[rows, :] = jnp.where(act > 0, acc, s["state"][rows, :]).astype(BF)

    def norm_bwd(dn, g, z, rstd, gi):
        e = dn * g
        gs[gi : gi + 1, :] += jnp.sum(dn * z, axis=0, keepdims=True)
        gs[gi + 1 : gi + 2, :] += jnp.sum(dn, axis=0, keepdims=True)
        m1 = jnp.mean(e, axis=1, keepdims=True)
        m2 = jnp.mean(e * z, axis=1, keepdims=True)
        return wide(rstd) * (e - m1 - z * m2)

    def backward_hidden(t, i):
        rows = pl.ds(pl.multiple_of(i * C, C), C)
        if t == 1:
            br = jnp.where(wide(s["act"][rows, :]) > 0, cot[rows, :].astype(F32), 0.0)
        else:
            br = s["state"][rows, :]
        b2 = br.astype(BF)
        gs[4:5, :] += jnp.sum(br, axis=0, keepdims=True)
        b2t = b2.T
        n2t = s["n2"][t, rows, :].T
        dn2 = jnp.zeros((C, D), F32)
        for c in range(4):
            G[WD + c] += dot(b2t, s["h"][t, c, rows, :])
            dp = s["d"][t, c, rows, :].astype(F32) * dot(b2, W(WD + c))
            gs[5 + c : 6 + c, :] += jnp.sum(dp, axis=0, keepdims=True)
            dp = dp.astype(BF)
            G[WU + c] += dot(n2t, dp)
            dn2 = dn2 + dot(dp, W(WU + c), NT)
        bres = br + norm_bwd(dn2, small[2:3, :], s["z2"][t, rows, :], s["r2"][t, rows, :], 2)
        s["bres"][rows, :] = bres
        b1 = bres.astype(BF)
        G[WO] += dot(b1.T, s["at"][t, rows, :])
        s["do"][rows, :] = dot(b1, W(WO)).astype(BF)

    def backward_attention(t, i):
        r0 = pl.multiple_of(i * C, C)
        rows = pl.ds(r0, C)
        for u in reversed(range(C // QB)):
            b = i * (C // QB) + u
            win = pl.ds(pl.multiple_of(b * QB, QB), 2 * QB)
            qrows = pl.ds(pl.multiple_of(b * QB, QB), QB)
            kw, vw = s["k"][t, win, :], s["v"][t, win, :]
            qb, dob = s["q"][t, qrows, :], s["do"][qrows, :]
            qs = jnp.concatenate([qb * hm[h] for h in range(HEADS)], axis=0)
            dos = jnp.concatenate([dob * hm[h] for h in range(HEADS)], axis=0)
            p = s["p"][t, b]
            dp = dot(dos, vw, NT)
            pf = p.astype(F32)
            tt = pf * dp
            ds_ = (tt - pf * jnp.sum(tt, axis=1, keepdims=True)).astype(BF)
            dq = dot(ds_, kw)
            a = dq[0:QB]
            for h in range(1, HEADS):
                a = jnp.where(lane_head == h, dq[h * QB : (h + 1) * QB], a)
            s["dq"][pl.ds(u * QB, QB), :] = (a * (D // HEADS) ** -0.5).astype(BF)
            s["dv"][win, :] += dot(p, dos, TN)
            s["dk"][win, :] += dot(ds_, qs, TN)
        dq = s["dq"][...]
        own_keys = pl.ds(r0 + QB, C)
        dk = (s["dk"][own_keys, :] * (D // HEADS) ** -0.5).astype(BF)
        dv = s["dv"][own_keys, :].astype(BF)
        n1t = s["n1"][t, rows, :].T
        G[WQ] += dot(n1t, dq)
        G[WK] += dot(n1t, dk)
        G[WV] += dot(n1t, dv)
        dn1 = dot(dq, W(WQ), NT) + dot(dk, W(WK), NT) + dot(dv, W(WV), NT)
        bm = s["bres"][rows, :] + norm_bwd(dn1, small[0:1, :], s["z1"][t, rows, :], s["r1"][t, rows, :], 0)
        if t == 1:
            s["bi"][rows, :] = bm
            s["state"][rows, :] = jnp.where(wide(s["act"][rows, :]) > 0, 0.0, cot[rows, :].astype(F32)) + bm
        else:
            ing[rows, :] = (s["bi"][rows, :] + 2.0 * bm).astype(BF)

    return forward_attention, forward_hidden, backward_hidden, backward_attention


def body(names, line, plane, r, *refs):
    s = dict(zip(names, refs))
    res, wb, G, gs, small = s["res"], s["wb"], s["G"], s["gs"], s["small"]
    gb = s.get("gb", wb)
    S, D = s["tok"].shape
    n = line * plane
    rp = wb.shape[3]
    x = Exchange(line, plane)
    core, me = x.core, x.me

    barrier = pltpu.get_barrier_semaphore()
    pl.semaphore_signal(barrier, inc=1, device_id=x.sibling(), device_id_type=MESH)
    for k in range(1, n):
        pl.semaphore_signal(
            barrier,
            inc=1,
            device_id={"dp": core, "wide": lax.rem(me + k, n)},
            device_id_type=MESH,
        )

    lanes = lax.broadcasted_iota(jnp.int32, (16, D), 1)
    rows16 = lax.broadcasted_iota(jnp.int32, (16, D), 0)
    tile = s["tile"]
    tile[...] = jnp.zeros((16, D), F32)
    for i, key in enumerate(("g1", "s1", "g2", "s2", "bd")):
        tile[i : i + 1, 0:r] = s[key][...].astype(F32)
    own = pltpu.roll(tile[...], me * r, axis=1)
    tile[0:1, 0 : 4 * r] = s["bu"][...].astype(F32)
    ups = jnp.broadcast_to(tile[0:1, :], (16, D))
    ups = jnp.where((lanes < 4 * r) & (rows16 == 5 + (me * 4 * r) // D), ups, 0.0)
    small_own = jnp.where(rows16 < 5, own, pltpu.roll(ups, lax.rem(me * 4 * r, D), axis=1)).astype(BF)
    first = jnp.where(core == 0, 1.0, 0.0).astype(BF)
    second = jnp.where(core == 0, 0.0, 1.0).astype(BF)

    def pad(v):
        return v if rp == r else jnp.concatenate([v.astype(F32), jnp.zeros((rp - r, D), F32)], axis=0).astype(BF)

    up = [pad(s["up"][:, c * D : (c + 1) * D]) for c in range(4)]
    down = [pad(s["down"][:, c * D : (c + 1) * D]) for c in range(4)]
    q_own, k_own, v_own, o_own = (pad(s[key][...]) for key in ("wq", "wk", "wv", "wo"))
    for (base, half), parts in (
        (GROUP_A, ((small_own, k_own), (q_own, v_own))),
        (GROUP_B, ((o_own, up[2]), (up[0], up[3]), (up[1], up[3]))),
        (GROUP_C, ((down[0], down[2]), (down[1], down[3]))),
    ):
        for i, (of_first, of_second) in enumerate(parts):
            wb[base + half * core + i, x.a, x.p] = of_first * first + of_second * second

    layout(s)

    pl.semaphore_wait(barrier, n)

    def mine(group, buf=wb):
        base, half = group
        return buf.at[pl.ds(base + half * core, half)]

    sem = {key: (s["send_" + key], s["recv_" + key]) for key in SEMS(line, plane)}
    to_a = [
        send(mine(GROUP_A).at[:, x.a, x.p], mine(GROUP_A).at[:, x.a, x.p], sem["a"], k - 1,
             {"dp": core, "wide": lax.rem(me + k, n)})
        for k in range(1, n)
    ]
    to_b = [
        send(mine(GROUP_B).at[:, x.a, x.p], mine(GROUP_B).at[:, x.a, x.p], sem["b1"], k - 1,
             x.chip(x.along(k), x.p))
        for k in range(1, line)
    ]
    to_c = [
        send(mine(GROUP_C).at[:, x.a, x.p], mine(GROUP_C).at[:, x.a, x.p], sem["c1"], k - 1,
             x.chip(x.a, x.across(k)))
        for k in range(1, plane)
    ]
    arrived(to_a)
    share_a = [send(mine(GROUP_A), mine(GROUP_A), sem["sib"], 0, x.sibling())]
    arrived(to_b)
    to_b2 = [
        send(mine(GROUP_B).at[:, :, x.p], mine(GROUP_B).at[:, :, x.p], sem["b2"], k - 1,
             x.chip(x.a, x.across(k)))
        for k in range(1, plane)
    ]
    arrived(to_c)
    to_c2 = [
        send(mine(GROUP_C).at[:, x.a], mine(GROUP_C).at[:, x.a], sem["c2"], k - 1,
             x.chip(x.along(k), x.p))
        for k in range(1, line)
    ]
    arrived(share_a)
    whole_small = wb[SMALL].reshape(n, rp, D).astype(F32)
    small[...] = jnp.sum(whole_small, axis=0)[0:16]

    def W(i):
        return wb[i].reshape(D, D) if rp == r else s["wf"][i]

    def places():
        row = lax.broadcasted_iota(jnp.int32, (D, n * rp), 0)
        place = lax.broadcasted_iota(jnp.int32, (D, n * rp), 1)
        return jnp.where(place == (row // r) * rp + lax.rem(row, r), 1.0, 0.0).astype(BF)

    def unpack(base, count):
        if rp != r:

            @pl.loop(base, base + count)
            def _(i):
                s["wf"][i] = dot(places(), wb[i].reshape(n * rp, D)).astype(BF)

    C = s["dq"].shape[0]
    forward_attention, forward_hidden, backward_hidden, backward_attention = block(s, W, C)

    def chunks(*steps):
        def one(i):
            for step, t in steps:
                step(t, S // C - 1 - i if step in (backward_hidden, backward_attention) else i)

        if S == C:
            one(0)
        else:
            pl.loop(0, S // C)(one)

    unpack(WQ, 3)

    chunks((forward_attention, 0))

    arrived(to_b2)
    share_b = [send(mine(GROUP_B), mine(GROUP_B), sem["sib"], 1, x.sibling())]
    arrived(to_c2)
    share_c = [send(mine(GROUP_C), mine(GROUP_C), sem["sib"], 2, x.sibling())]
    arrived(share_b + share_c)
    unpack(WO, 5)
    unpack(WD, 4)

    chunks((forward_hidden, 0))
    chunks((forward_attention, 1), (forward_hidden, 1))

    s["dk"][...] = jnp.zeros(s["dk"].shape, F32)
    s["dv"][...] = jnp.zeros(s["dv"].shape, F32)

    chunks((backward_hidden, 1), (backward_attention, 1))
    chunks((backward_hidden, 0))

    def stage(base, count):
        @pl.loop(base, base + count)
        def _(i):
            if rp == r:
                gb[i] = G[i].astype(BF).reshape(line, plane, r, D)
            else:
                gb[i] = dot(places(), G[i].astype(BF), TN).astype(BF).reshape(line, plane, rp, D)

    def swap(group, inbox, k):
        base, half = group
        return [send(gb.at[pl.ds(base + half * (1 - core), half)], inbox, sem["rsib"], k, x.sibling())]

    def add_swapped(copies, group, inbox):
        arrived(copies)
        base, half = group
        @pl.loop(0, half)
        def _(i):
            at = base + half * core + i
            gb[at] = (gb[at].astype(F32) + inbox[i].astype(F32)).astype(BF)

    def finished(group, k, total):
        base, half = group
        for i in range(half):
            res[base + half * core + i] = total[i]
        part = res.at[pl.ds(base + half * core, half)]
        return [send(part, part, sem["fsib"], k, x.sibling())]

    left(to_a + to_b + to_c + to_b2 + to_c2 + share_a + share_b + share_c)
    stage(WO, 5)
    gb[WO + 5] = jnp.zeros(gb.shape[1:], BF)
    stage(WD, 4)
    swap_b = swap(GROUP_B, s["inb"], 1)
    swap_c = swap(GROUP_C, s["inc"], 2)

    s["dk"][...] = jnp.zeros(s["dk"].shape, F32)
    s["dv"][...] = jnp.zeros(s["dv"].shape, F32)
    add_swapped(swap_b, GROUP_B, s["inb"])
    from_b = [
        send(mine(GROUP_B, gb).at[:, :, x.across(k)], s["inb1"].at[k - 1], sem["rb1"], k - 1,
             x.chip(x.a, x.across(k)))
        for k in range(1, plane)
    ]
    add_swapped(swap_c, GROUP_C, s["inc"])
    from_c = [
        send(mine(GROUP_C, gb).at[:, x.along(k)], s["inc1"].at[k - 1], sem["rc1"], k - 1,
             x.chip(x.along(k), x.p))
        for k in range(1, line)
    ]
    chunks((backward_attention, 0))
    stage(WQ, 3)
    gb[SMALL] = jnp.broadcast_to(gs[...].astype(BF)[None, None], (line, plane, 16, D))
    swap_a = swap(GROUP_A, s["ina"], 0)
    arrived(from_b)
    sum_b = mine(GROUP_B, gb)[:, :, x.p].astype(F32)
    for k in range(1, plane):
        sum_b = sum_b + s["inb1"][k - 1].astype(F32)
    s["sumb"][...] = sum_b.astype(BF)
    from_b2 = [
        send(s["sumb"].at[:, x.along(k)], s["inb2"].at[k - 1], sem["rb2"], k - 1, x.chip(x.along(k), x.p))
        for k in range(1, line)
    ]
    arrived(from_c)
    sum_c = mine(GROUP_C, gb)[:, x.a].astype(F32)
    for k in range(1, line):
        sum_c = sum_c + s["inc1"][k - 1].astype(F32)
    s["sumc"][...] = sum_c.astype(BF)
    from_c2 = [
        send(s["sumc"].at[:, x.across(k)], s["inc2"].at[k - 1], sem["rc2"], k - 1, x.chip(x.a, x.across(k)))
        for k in range(1, plane)
    ]
    add_swapped(swap_a, GROUP_A, s["ina"])
    from_a = []
    for k in range(1, n):
        to = lax.rem(me + k, n)
        from_a.append(
            send(mine(GROUP_A, gb).at[:, to // plane, lax.rem(to, plane)], s["ina1"].at[k - 1], sem["ra"], k - 1,
                 {"dp": core, "wide": to})
        )
    arrived(from_b2)
    total = s["sumb"][:, x.a].astype(F32)
    for k in range(1, line):
        total = total + s["inb2"][k - 1].astype(F32)
    done_b = finished(GROUP_B, 1, total)
    arrived(from_c2)
    total = s["sumc"][:, x.p].astype(F32)
    for k in range(1, plane):
        total = total + s["inc2"][k - 1].astype(F32)
    done_c = finished(GROUP_C, 2, total)
    arrived(from_a)
    total = mine(GROUP_A, gb)[:, x.a, x.p].astype(F32)
    for k in range(1, n):
        total = total + s["ina1"][k - 1].astype(F32)
    done_a = finished(GROUP_A, 0, total)
    arrived(done_a + done_b + done_c)
    left(swap_a + swap_b + swap_c + from_a + from_b + from_b2 + from_c + from_c2)
    left(done_a + done_b + done_c)


def SEMS(line, plane):
    n = line * plane
    return {
        "a": n - 1, "b1": line - 1, "c1": plane - 1, "b2": plane - 1, "c2": line - 1, "sib": 3,
        "rsib": 3, "rb1": plane - 1, "rb2": line - 1, "rc1": line - 1, "rc2": plane - 1, "ra": n - 1, "fsib": 3,
    }


def scratch(S, D, line, plane, rp):
    nb, n = S // QB, line * plane
    V = pltpu.VMEM
    C = S if D // n == rp else 256
    shapes = dict(
        tile=V((16, D), F32), small=V((16, D), F32),
        wb=V((SLABS, line, plane, rp, D), BF),
        G=V((SLABS, D, D), F32), gs=V((16, D), F32),
        ina=V((2, line, plane, rp, D), BF), inb=V((3, line, plane, rp, D), BF), inc=V((2, line, plane, rp, D), BF),
        ina1=V((n - 1, 2, rp, D), BF),
        inb1=V((plane - 1, 3, line, rp, D), BF), inb2=V((line - 1, 3, rp, D), BF), sumb=V((3, line, rp, D), BF),
        inc1=V((line - 1, 2, plane, rp, D), BF), inc2=V((plane - 1, 2, rp, D), BF), sumc=V((2, plane, rp, D), BF),
        mask=V((nb, QB, 2 * QB), F32), act=V((S, 128), F32), state=V((S, D), F32), mixed=V((S, D), F32),
        z1=V((2, S, D), F32), r1=V((2, S, 128), F32), n1=V((2, S, D), BF),
        z2=V((2, S, D), F32), r2=V((2, S, 128), F32), n2=V((2, S, D), BF),
        q=V((2, S, D), BF), k=V((2, S + QB, D), BF), v=V((2, S + QB, D), BF),
        p=V((2, nb, HEADS * QB, 2 * QB), BF), at=V((2, S, D), BF),
        h=V((2, 4, S, D), BF), d=V((2, 4, S, D), BF),
        bres=V((S, D), F32), do=V((S, D), BF),
        dq=V((C, D), BF), dk=V((S + QB, D), F32), dv=V((S + QB, D), F32), bi=V((S, D), F32),
    )
    if D // n != rp:
        shapes["wf"] = V((SLABS, D, D), BF)
    else:
        shapes["gb"] = V((SLABS, line, plane, rp, D), BF)
    for key, count in SEMS(line, plane).items():
        shapes["send_" + key] = pltpu.SemaphoreType.DMA((count,))
        shapes["recv_" + key] = pltpu.SemaphoreType.DMA((count,))
    return shapes


def finish(r, *refs):
    out_in, ing_in, res, out, ing, gq, gk, gv, go, gu, gd, gg1, gs1, gg2, gs2, gbu, gbd = refs
    out[...] = out_in[...]
    ing[...] = ing_in[...]
    D = res.shape[2]
    me = lax.axis_index("wide")
    for ref, at in ((gq, WQ), (gk, WK), (gv, WV), (go, WO)):
        ref[...] = res[at, 0:r, :]
    for c in range(4):
        gu[:, c * D : (c + 1) * D] = res[WU + c, 0:r, :]
        gd[:, c * D : (c + 1) * D] = res[WD + c, 0:r, :]
    tile = res[SMALL, 0:16, :]
    own = pltpu.roll(tile, lax.rem(D - me * r, D), axis=1)
    for i, ref in enumerate((gg1, gs1, gg2, gs2, gbd)):
        ref[...] = own[i : i + 1, 0:r]
    row = jnp.zeros((1, D), F32)
    for c in range(4):
        row = jnp.where((me * 4 * r) // D == c, tile[5 + c : 6 + c, :], row)
    row = jnp.broadcast_to(row, (8, D))
    gbu[...] = pltpu.roll(row, lax.rem(D - lax.rem(me * 4 * r, D), D), axis=1)[0:1, 0 : 4 * r]


def on_device(sizes, *args):
    (tokens, lengths, counts, wq, wk, wv, wo, wu, wd, g1, s1, g2, s2, bu, bd, cot) = args
    line, plane = sizes
    S, D = tokens.shape[1:]
    r = wq.shape[0]
    rp = max(r, 16)
    vm = pl.BlockSpec(memory_space=pltpu.VMEM)
    sm = pl.BlockSpec(memory_space=pltpu.SMEM)
    inputs = dict(
        tok=tokens[0], cot=cot[0], lens=lengths, cnts=counts, wq=wq, wk=wk, wv=wv, wo=wo.T, up=wu, down=wd.T,
        g1=g1[None], s1=s1[None], g2=g2[None], s2=s2[None], bu=bu[None], bd=bd[None],
    )
    shapes = scratch(S, D, line, plane, rp)
    names = [*inputs, "out", "ing", "res", *shapes]
    out, ing, res = pl.pallas_call(
        functools.partial(body, names, line, plane, r),
        out_shape=(
            jax.ShapeDtypeStruct((S, D), BF),
            jax.ShapeDtypeStruct((S, D), BF),
            jax.ShapeDtypeStruct((SLABS, rp, D), F32),
        ),
        in_specs=[sm if key in ("lens", "cnts") else vm for key in inputs],
        out_specs=(vm, vm, vm),
        scratch_shapes=list(shapes.values()),
        compiler_params=pltpu.CompilerParams(
            collective_id=0, has_side_effects=True, vmem_limit_bytes=60 * 2**20
        ),
        name="loop_block",
    )(*inputs.values())
    f = lambda *shape: jax.ShapeDtypeStruct(shape, F32)
    out, ing, gq, gk, gv, go, gu, gd, gg1, gs1, gg2, gs2, gbu, gbd = pl.pallas_call(
        functools.partial(finish, r),
        out_shape=(
            jax.ShapeDtypeStruct((S, D), BF), jax.ShapeDtypeStruct((S, D), BF),
            f(r, D), f(r, D), f(r, D), f(r, D), f(r, 4 * D), f(r, 4 * D),
            f(1, r), f(1, r), f(1, r), f(1, r), f(1, 4 * r), f(1, r),
        ),
        in_specs=[vm] * 3,
        out_specs=(vm,) * 14,
        name="finish",
    )(out, ing, res)
    return (out[None], ing[None], gq, gk, gv, go.T, gu, gd.T, gg1[0], gs1[0], gg2[0], gs2[0], gbu[0], gbd[0])


def solution(mesh):
    wide = mesh.shape["wide"]
    line = 4 if wide % 4 == 0 else 1
    rows = P(("dp", "wide"), None, None)
    row = P(("dp", "wide"), None)
    first, second, one = P("wide", None), P(None, "wide"), P("wide")
    weights = (first, first, first, second, first, second)
    return jax.shard_map(
        functools.partial(on_device, (line, wide // line)),
        mesh=mesh,
        in_specs=(rows, row, row, *weights, *(one,) * 6, rows),
        out_specs=(rows, rows, *weights, *(one,) * 6),
        check_vma=False,
    )
```

```python
import functools
import math

import jax
import jax.numpy as jnp
from jax import lax
from jax.experimental import pallas as pl
from jax.experimental.pallas import tpu as pltpu
from jax.sharding import PartitionSpec as P

F32, BF = jnp.float32, jnp.bfloat16
MESH = pl.DeviceIdType.MESH
HEADS = 4
NORM_EPS = 1e-05
MASK_FILL = -1e30
QB = 128
NN = (((1,), (0,)), ((), ()))
NT = (((1,), (1,)), ((), ()))
TN = (((0,), (0,)), ((), ()))
C0 = math.sqrt(2 / math.pi)
C1 = C0 * 0.044715

SMALL, WQ, WK, WV, WO, WU, WD = 0, 1, 2, 3, 4, 5, 10
SLABS = 14
GROUP_A, GROUP_B, GROUP_C = (0, 2), (4, 3), (10, 2)


def dot(a, b, dims=NN):
    return lax.dot_general(a, b, dims, preferred_element_type=F32)


FETCHED = ("lens", "cnts", "wq", "wk", "wv", "wo", "up", "down", "g1", "s1", "g2", "s2", "bu", "bd")


class Exchange:
    def __init__(self, line, plane):
        self.line, self.plane = line, plane
        self.n = line * plane
        self.core = lax.axis_index("dp")
        self.me = lax.axis_index("wide")
        self.a = self.me // plane
        self.p = self.me % plane

    def chip(self, a, p):
        return {"dp": self.core, "wide": a * self.plane + p}

    def sibling(self):
        return {"dp": 1 - self.core, "wide": self.me}

    def along(self, step):
        return lax.rem(self.a + step, self.line)

    def across(self, step):
        return lax.rem(self.p + step, self.plane)


class Copies:
    def __init__(self, sems, k, size):
        self.send_sem, self.recv_sem, self.size = sems[0].at[k], sems[1].at[k], size

    def start(self, src, dst, device):
        pltpu.make_async_remote_copy(
            src_ref=src,
            dst_ref=dst,
            send_sem=self.send_sem,
            recv_sem=self.recv_sem,
            device_id=device,
            device_id_type=MESH,
        ).start()

    def arrived(self):
        pltpu.make_async_copy(self.size, self.size, self.recv_sem).wait()

    def left(self):
        pltpu.make_async_copy(self.size, self.size, self.send_sem).wait()


def arrived(*copies):
    for copy in copies:
        copy.arrived()


def left(*copies):
    for copy in copies:
        copy.left()


def layout(s):
    lens, cnts, G, gs = s["lens"], s["cnts"], s["G"], s["gs"]
    S, D = s["tok"].shape
    nb = S // QB
    slot = lax.broadcasted_iota(jnp.int32, (nb, QB), 0) * QB + lax.broadcasted_iota(jnp.int32, (nb, QB), 1)
    end = jnp.int32(0)
    start_of = jnp.zeros((nb, QB), jnp.int32)
    loops_of = jnp.zeros((nb, QB), jnp.int32)
    for j in range(lens.shape[1]):
        inside = slot >= end
        start_of = jnp.where(inside, end, start_of)
        loops_of = jnp.where(inside, cnts[0, j], loops_of)
        end = end + lens[0, j]
    start_t = jnp.transpose(start_of.astype(F32))
    loops_t = jnp.transpose(loops_of.astype(F32))
    kk = lax.broadcasted_iota(jnp.int32, (QB, 2 * QB), 1).astype(F32)
    qq = lax.broadcasted_iota(jnp.int32, (QB, 2 * QB), 0).astype(F32)
    for b in range(nb):
        ok = (kk >= start_t[:, b : b + 1] - (b - 1) * QB) & (kk <= qq + QB)
        if b == 0:
            ok = ok & (kk >= QB)
        s["mask"][b] = jnp.where(ok, 0.0, MASK_FILL)
        s["act"][pl.ds(b * QB, QB), :] = jnp.broadcast_to(
            jnp.where(loops_t[:, b : b + 1] > 1, 1.0, 0.0), (QB, 128)
        )
    for t in range(2):
        s["k"][t, 0:QB, :] = jnp.zeros((QB, D), BF)
        s["v"][t, 0:QB, :] = jnp.zeros((QB, D), BF)
    G[...] = jnp.zeros(G.shape, F32)
    gs[...] = jnp.zeros(gs.shape, F32)


def no_keys_ahead(s):
    for key in ("dk", "dv"):
        ref = s[key]
        ref[pl.ds(ref.shape[0] - QB, QB), :] = jnp.zeros((QB, ref.shape[1]), F32)


def block(s, W, C):
    tok, cot, out, ing, small, G, gs = (s[key] for key in ("tok", "cot", "out", "ing", "small", "G", "gs"))
    D = tok.shape[1]
    scale = (D // HEADS) ** -0.5
    lane_head = lax.broadcasted_iota(jnp.int32, (1, D), 1) // (D // HEADS)
    hm = [jnp.where(lane_head == h, 1.0, 0.0).astype(BF) for h in range(HEADS)]

    def wide(v):
        return jnp.concatenate([v, v], axis=1)

    def by_head(v):
        return jnp.concatenate([v * hm[h] for h in range(HEADS)], axis=0)

    def of_heads(v):
        own = v[0:QB]
        for h in range(1, HEADS):
            own = jnp.where(lane_head == h, v[h * QB : (h + 1) * QB], own)
        return own

    def block_rows(b):
        at = lambda k, size: pl.ds(pl.multiple_of(k * QB, QB), size)
        return at(b, 2 * QB), at(b, QB), at(b + 1, QB)

    def normalized(v):
        mean = jnp.mean(v, axis=1, keepdims=True)
        cen = v - mean
        var = jnp.mean(cen * cen, axis=1, keepdims=True)
        rstd = lax.rsqrt(var + NORM_EPS)
        return cen * rstd, jnp.broadcast_to(rstd, (C, 128))

    def add(ref, at, t, value):
        if t == 1 and C == tok.shape[0]:
            ref[at] = value
        else:
            ref[at] += value

    def forward_mixed(t, i):
        rows = pl.ds(pl.multiple_of(i * C, C), C)
        tk = tok[rows, :].astype(F32)
        mixed = tk + tk if t == 0 else s["state"][rows, :] + tk
        s["mixed"][rows, :] = mixed
        s["z1"][t, rows, :], s["r1"][t, rows, :] = normalized(mixed)

    def forward_attention(t, i):
        r0 = pl.multiple_of(i * C, C)
        rows = pl.ds(r0, C)
        n1 = (s["z1"][t, rows, :] * small[0:1, :] + small[1:2, :]).astype(BF)
        s["n1"][t, rows, :] = n1
        q = dot(n1, W(WQ)).astype(BF)
        s["q"][t, rows, :] = q
        s["k"][t, pl.ds(r0 + QB, C), :] = dot(n1, W(WK)).astype(BF)
        s["v"][t, pl.ds(r0 + QB, C), :] = dot(n1, W(WV)).astype(BF)
        for u in range(C // QB):
            b = i * (C // QB) + u
            win = pl.ds(pl.multiple_of(b * QB, QB), 2 * QB)
            kw, vw = s["k"][t, win, :], s["v"][t, win, :]
            qb = q[u * QB : (u + 1) * QB]
            sc = dot(by_head(qb), kw, NT)
            mask = s["mask"][b]
            ps = []
            for h in range(HEADS):
                e = sc[h * QB : (h + 1) * QB] * scale + mask
                e = jnp.exp(e - jnp.max(e, axis=1, keepdims=True))
                ps.append((e * (1.0 / jnp.sum(e, axis=1, keepdims=True))).astype(BF))
            p = jnp.concatenate(ps, axis=0)
            s["p"][t, b] = p
            s["at"][t, pl.ds(pl.multiple_of(b * QB, QB), QB), :] = of_heads(dot(p, vw)).astype(BF)

    def forward_hidden(t, i):
        rows = pl.ds(pl.multiple_of(i * C, C), C)
        resid = s["mixed"][rows, :] + dot(s["at"][t, rows, :], W(WO), NT)
        z2, s["r2"][t, rows, :] = normalized(resid)
        s["z2"][t, rows, :] = z2
        n2 = (z2 * small[2:3, :] + small[3:4, :]).astype(BF)
        s["n2"][t, rows, :] = n2
        acc = resid + small[4:5, :]
        for c in range(4):
            hp = dot(n2, W(WU + c)) + small[5 + c : 6 + c, :]
            v2 = hp * hp
            th = jnp.tanh(hp * (C1 * v2 + C0))
            pr = 0.5 * th + 0.5
            g = hp * pr
            d = pr + g * (1.0 - pr) * ((6 * C1) * v2 + (2 * C0))
            g = g.astype(BF)
            s["h"][t, c, rows, :] = g
            s["d"][t, c, rows, :] = d.astype(BF)
            acc = acc + dot(g, W(WD + c), NT)
        if t == 0:
            s["state"][rows, :] = acc
        else:
            act = wide(s["act"][rows, :])
            out[rows, :] = jnp.where(act > 0, acc, s["state"][rows, :]).astype(BF)

    def norm_bwd(t, dn, g, z, rstd, gi):
        e = dn * g
        add(gs, slice(gi, gi + 1), t, jnp.sum(dn * z, axis=0, keepdims=True))
        add(gs, slice(gi + 1, gi + 2), t, jnp.sum(dn, axis=0, keepdims=True))
        m1 = jnp.mean(e, axis=1, keepdims=True)
        m2 = jnp.mean(e * z, axis=1, keepdims=True)
        return wide(rstd) * (e - m1 - z * m2)

    def back_renewed(t, rows):
        if t == 0:
            return s["state"][rows, :]
        return jnp.where(wide(s["act"][rows, :]) > 0, cot[rows, :].astype(F32), 0.0)

    def backward_hidden(t, i):
        rows = pl.ds(pl.multiple_of(i * C, C), C)
        br = back_renewed(t, rows)
        add(gs, slice(4, 5), t, jnp.sum(br, axis=0, keepdims=True))
        b2 = br.astype(BF)
        b2t = b2.T
        n2t = s["n2"][t, rows, :].T
        dn2 = jnp.zeros((C, D), F32)
        for c in range(4):
            add(G, WD + c, t, dot(b2t, s["h"][t, c, rows, :]))
            dp = s["d"][t, c, rows, :].astype(F32) * dot(b2, W(WD + c))
            add(gs, slice(5 + c, 6 + c), t, jnp.sum(dp, axis=0, keepdims=True))
            dp = dp.astype(BF)
            add(G, WU + c, t, dot(n2t, dp))
            dn2 = dn2 + dot(dp, W(WU + c), NT)
        bres = br + norm_bwd(t, dn2, small[2:3, :], s["z2"][t, rows, :], s["r2"][t, rows, :], 2)
        s["bres"][rows, :] = bres
        b1 = bres.astype(BF)
        add(G, WO, t, dot(b1.T, s["at"][t, rows, :]))
        s["do"][rows, :] = dot(b1, W(WO)).astype(BF)

    def backward_scores(t, i, blocks):
        for b in reversed(blocks):
            b = i * (C // QB) + b
            win, behind, ahead = block_rows(b)
            kw, vw = s["k"][t, win, :], s["v"][t, win, :]
            qs, dos = by_head(s["q"][t, behind, :]), by_head(s["do"][behind, :])
            p = s["p"][t, b]
            pf = p.astype(F32)
            tt = pf * dot(dos, vw, NT)
            ds = (tt - pf * jnp.sum(tt, axis=1, keepdims=True)).astype(BF)
            s["dq"][behind, :] = (of_heads(dot(ds, kw)) * scale).astype(BF)
            for ref, value in ((s["dv"], dot(p, dos, TN)), (s["dk"], dot(ds, qs, TN))):
                ref[behind, :] = value[0:QB]
                ref[ahead, :] += value[QB:]

    def backward_late(t, i):
        backward_scores(t, i, range(C // QB // 2, C // QB))

    def backward_early(t, i):
        backward_scores(t, i, range(C // QB // 2))
        rows = pl.ds(pl.multiple_of(i * C, C), C)
        own_keys = pl.ds(pl.multiple_of(i * C, C) + QB, C)
        n1t = s["n1"][t, rows, :].T
        add(G, WQ, t, dot(n1t, s["dq"][rows, :]))
        add(G, WK, t, dot(n1t, (s["dk"][own_keys, :] * scale).astype(BF)))
        add(G, WV, t, dot(n1t, s["dv"][own_keys, :].astype(BF)))

    def backward_mixed(t, i):
        r0 = pl.multiple_of(i * C, C)
        rows = pl.ds(r0, C)
        own_keys = pl.ds(r0 + QB, C)
        dn1 = dot(s["dq"][rows, :], W(WQ), NT)
        dn1 = dn1 + dot((s["dk"][own_keys, :] * scale).astype(BF), W(WK), NT)
        dn1 = dn1 + dot(s["dv"][own_keys, :].astype(BF), W(WV), NT)
        back = norm_bwd(t, dn1, small[0:1, :], s["z1"][t, rows, :], s["r1"][t, rows, :], 0)
        bm = s["bres"][rows, :] + back
        if t == 1:
            s["bi"][rows, :] = bm
            s["state"][rows, :] = jnp.where(wide(s["act"][rows, :]) > 0, 0.0, cot[rows, :].astype(F32)) + bm
        else:
            ing[rows, :] = (s["bi"][rows, :] + 2.0 * bm).astype(BF)

    forward = (forward_mixed, forward_attention, forward_hidden)
    return forward, (backward_hidden, backward_late, backward_early, backward_mixed)


def body(names, line, plane, r, *refs):
    s = dict(zip(names, refs))
    res, wb, G, gs, small = s["res"], s["wb"], s["G"], s["gs"], s["small"]
    gb = s.get("gb", wb)
    S, D = s["tok"].shape
    n = line * plane
    rp = wb.shape[3]
    x = Exchange(line, plane)
    core, me = x.core, x.me

    large = s["large"]
    fetch_tok = pltpu.make_async_copy(s["tok_hbm"], s["tok"], large.at[0])
    fetch_cot = pltpu.make_async_copy(s["cot_hbm"], s["cot"], large.at[1])
    store_out = pltpu.make_async_copy(s["out"], s["out_hbm"], large.at[2])
    store_ing = pltpu.make_async_copy(s["ing"], s["ing_hbm"], large.at[3])
    barrier = pltpu.get_barrier_semaphore()
    pl.semaphore_signal(barrier, inc=1, device_id=x.sibling(), device_id_type=MESH)
    for k in range(1, n):
        pl.semaphore_signal(
            barrier,
            inc=1,
            device_id={"dp": core, "wide": lax.rem(me + k, n)},
            device_id_type=MESH,
        )

    fetches = [
        pltpu.make_async_copy(s[key + "_hbm"], s[key], s["fetch"].at[i]) for i, key in enumerate(FETCHED)
    ]
    for copy in (*fetches, fetch_tok, fetch_cot):
        copy.start()
    for copy in fetches:
        copy.wait()

    for k in range(1, plane):
        device = {"dp": 1 - core, "wide": x.chip(x.a, x.across(k))["wide"]}
        pl.semaphore_signal(barrier, inc=1, device_id=device, device_id_type=MESH)

    lanes = lax.broadcasted_iota(jnp.int32, (16, D), 1)
    rows16 = lax.broadcasted_iota(jnp.int32, (16, D), 0)
    tile = s["tile"]
    tile[...] = jnp.zeros((16, D), F32)
    for i, key in enumerate(("g1", "s1", "g2", "s2", "bd")):
        tile[i : i + 1, 0:r] = s[key][...].astype(F32)
    own = pltpu.roll(tile[...], me * r, axis=1)
    tile[0:1, 0 : 4 * r] = s["bu"][...].astype(F32)
    ups = jnp.broadcast_to(tile[0:1, :], (16, D))
    ups = jnp.where((lanes < 4 * r) & (rows16 == 5 + (me * 4 * r) // D), ups, 0.0)
    small_own = jnp.where(rows16 < 5, own, pltpu.roll(ups, lax.rem(me * 4 * r, D), axis=1)).astype(BF)
    first = jnp.where(core == 0, 1.0, 0.0).astype(BF)
    second = jnp.where(core == 0, 0.0, 1.0).astype(BF)

    def pad(v):
        return v if rp == r else jnp.concatenate([v.astype(F32), jnp.zeros((rp - r, D), F32)], axis=0).astype(BF)

    up = [pad(s["up"][:, c * D : (c + 1) * D]) for c in range(4)]
    down = [pad(s["down"][:, c * D : (c + 1) * D]) for c in range(4)]
    q_own, k_own, v_own, o_own = (pad(s[key][...]) for key in ("wq", "wk", "wv", "wo"))
    for (base, half), parts in (
        (GROUP_A, ((small_own, k_own), (q_own, v_own))),
        (GROUP_B, ((o_own, up[2]), (up[0], up[3]), (up[1], up[3]))),
        (GROUP_C, ((down[0], down[2]), (down[1], down[3]))),
    ):
        for i, (of_first, of_second) in enumerate(parts):
            wb[base + half * core + i, x.a, x.p] = of_first * first + of_second * second

    layout(s)

    def W(i):
        return wb[i].reshape(D, D) if rp == r else s["wf"][i]

    def places():
        row = lax.broadcasted_iota(jnp.int32, (D, n * rp), 0)
        place = lax.broadcasted_iota(jnp.int32, (D, n * rp), 1)
        return jnp.where(place == (row // r) * rp + lax.rem(row, r), 1.0, 0.0).astype(BF)

    def unpack(base, count):
        if rp != r:

            @pl.loop(base, base + count)
            def _(i):
                s["wf"][i] = dot(places(), wb[i].reshape(n * rp, D)).astype(BF)

    C = S if rp == r else 256
    forward, backward = block(s, W, C)
    forward_mixed, forward_attention, forward_hidden = forward
    backward_hidden, backward_late, backward_early, backward_mixed = backward

    def chunks(t, *steps):
        def one(i):
            for step in steps:
                step(t, S // C - 1 - i if step in backward else i)

        if S == C:
            one(0)
        else:
            pl.loop(0, S // C)(one)

    fetch_tok.wait()
    chunks(0, forward_mixed)

    def mine(group):
        base, half = group
        return wb.at[pl.ds(base + half * core, half)]

    def start_all(k, size, sends):
        copies = Copies((s["send"], s["recv"]), k, size)
        for send in sends:
            copies.start(*send)
        return copies

    def along_line(k, size, ref, inbox):
        return start_all(k, size, [(ref(x.along(i)), inbox(i), x.chip(x.along(i), x.p)) for i in range(1, line)])

    def across_plane(k, size, ref, inbox):
        return start_all(k, size, [(ref(x.across(i)), inbox(i), x.chip(x.a, x.across(i))) for i in range(1, plane)])

    def to_sibling(k, size, src, dst):
        return start_all(k, size, [(src, dst, x.sibling())])

    def share(k, group):
        return to_sibling(k, mine(group), mine(group), mine(group))

    def bytes_of(group, devices):
        return s["size"].at[pl.ds(0, group[1]), pl.ds(0, devices)]

    pl.semaphore_wait(barrier, n + plane - 1)
    own_b, own_c = (mine(group).at[:, x.a, x.p] for group in (GROUP_B, GROUP_C))
    to_b = along_line(0, bytes_of(GROUP_B, line - 1), lambda _: own_b, lambda _: own_b)
    to_c = along_line(1, bytes_of(GROUP_C, line - 1), lambda _: own_c, lambda _: own_c)
    own_a = mine(GROUP_A).at[:, x.a, x.p]
    everyone = [{"dp": core, "wide": lax.rem(me + k, n)} for k in range(1, n)]
    to_a = start_all(2, bytes_of(GROUP_A, n - 1), [(own_a, own_a, device) for device in everyone])
    arrived(to_b)
    line_b, line_c = (mine(group).at[:, :, x.p] for group in (GROUP_B, GROUP_C))
    to_b2 = across_plane(3, bytes_of(GROUP_B, line * (plane - 1)), lambda _: line_b, lambda _: line_b)
    arrived(to_c)
    to_c2 = across_plane(4, bytes_of(GROUP_C, line * (plane - 1)), lambda _: line_c, lambda _: line_c)
    arrived(to_a)
    share_a = share(5, GROUP_A)
    arrived(share_a)
    small[...] = jnp.sum(wb[SMALL].reshape(n, rp, D).astype(F32), axis=0)[0:16]
    unpack(WQ, 3)
    chunks(0, forward_attention)
    arrived(to_b2)
    share_b = share(6, GROUP_B)
    arrived(to_c2)
    share_c = share(7, GROUP_C)
    arrived(share_b, share_c)
    unpack(WO, 5)
    unpack(WD, 4)
    chunks(0, forward_hidden)
    chunks(1, forward_mixed, forward_attention, forward_hidden)

    store_out.start()
    fetch_cot.wait()
    no_keys_ahead(s)
    chunks(1, *backward)

    def blocks(i):
        if rp == r:
            return G[i].astype(BF).reshape(line, plane, r, D)
        return dot(places(), G[i].astype(BF), TN).astype(BF).reshape(line, plane, rp, D)

    def stage(first_slab, *weights):
        for k, i in enumerate(weights):
            gb[first_slab + k] = blocks(i)

    def kept(ref):
        half = ref.shape[0] // 2
        return ref.at[pl.ds(half * core, half)]

    def swap(k, ref, inbox):
        half = ref.shape[0] // 2
        return to_sibling(k, inbox, ref.at[pl.ds(half * (1 - core), half)], inbox)

    def add_swapped(copies, ref, inbox):
        arrived(copies)
        own = kept(ref)

        def one(i):
            own[i] = (own[i].astype(F32) + inbox[i].astype(F32)).astype(BF)

        pl.loop(0, own.shape[0])(one)

    def total(own, inbox):
        own = own.astype(F32)
        for k in range(inbox.shape[0]):
            own = own + inbox[k].astype(F32)
        return own

    def finished(k, ref, sums):
        part = kept(ref)
        part[...] = sums
        return to_sibling(k, part, part, part)

    def straight(k, ref, inbox):
        sends = []
        for i in range(n - 1):
            to = i + jnp.where(i >= me, 1, 0)
            device = {"dp": core, "wide": to}
            sends.append((kept(ref).at[:, to // plane, lax.rem(to, plane)], inbox.at[me - jnp.where(me > to, 1, 0)], device))
        return start_all(k, inbox, sends)

    def summed(ref, own, inbox):
        ref[...] = total(own, inbox).astype(BF)
        return ref

    left(to_a, to_b, to_c, to_b2, to_c2, share_a, share_b, share_c)
    gb_u, gb_d, gb_q = gb.at[pl.ds(0, 6)], gb.at[pl.ds(6, 4)], s["gq"]
    res_q, res_u, res_d = s["resq"], res.at[pl.ds(0, 6)], res.at[pl.ds(6, 4)]

    chunks(0, backward_hidden)
    stage(6, WD, WD + 1, WD + 2, WD + 3)
    swap_d = swap(8, gb_d, s["ind"])
    stage(0, WO, WU, WU + 1, WU + 2, WU + 3)
    gb[5] = jnp.zeros(gb.shape[1:], BF)
    swap_u = swap(9, gb_u, s["inu"])
    no_keys_ahead(s)
    chunks(0, backward_late)
    add_swapped(swap_d, gb_d, s["ind"])
    from_d = along_line(10, s["in1d"], lambda a: kept(gb_d).at[:, a], lambda i: s["in1d"].at[i - 1])
    add_swapped(swap_u, gb_u, s["inu"])
    from_u = across_plane(11, s["in1u"], lambda p: kept(gb_u).at[:, :, p], lambda i: s["in1u"].at[i - 1])
    chunks(0, backward_early)
    gb_q[0, :, :, :, 0:D] = blocks(WQ)
    gb_q[1, :, :, :, 0:D] = blocks(WK)
    value_blocks = blocks(WV)
    for c in range(2):
        gb_q[c, :, :, :, pl.ds(D, 128)] = value_blocks[:, :, :, 128 * c : 128 * (c + 1)]
    swap_q = swap(15, gb_q, s["inq"])
    chunks(0, backward_mixed)
    store_ing.start()
    vectors = s["vectors"]
    vectors[...] = gs[...].astype(BF)
    near = [{"dp": other, "wide": x.chip(x.a, x.across(i))["wide"]} for other in (core, 1 - core) for i in range(plane)]
    from_v = start_all(23, s["inv"], [(vectors, s["inv"].at[i], device) for i, device in enumerate(near[1:])])
    add_swapped(swap_q, gb_q, s["inq"])
    from_q = straight(16, gb_q, s["intq"])
    arrived(from_d)
    sumd = summed(s["sumd"], kept(gb_d)[:, x.a], s["in1d"])
    from_d2 = across_plane(14, s["in2d"], lambda p: sumd.at[:, p], lambda i: s["in2d"].at[i - 1])
    arrived(from_u)
    sumu = summed(s["sumu"], kept(gb_u)[:, :, x.p], s["in1u"])
    from_u2 = along_line(17, s["in2u"], lambda a: sumu.at[:, a], lambda i: s["in2u"].at[i - 1])
    arrived(from_v)
    sumv = summed(s["sumv"], vectors[...], s["inv"])
    from_v2 = along_line(24, s["in2v"], lambda _: sumv, lambda i: s["in2v"].at[i - 1])
    arrived(from_d2)
    done_d = finished(18, res_d, total(sumd[:, x.p], s["in2d"]))
    arrived(from_u2)
    done_u = finished(20, res_u, total(sumu[:, x.a], s["in2u"]))
    arrived(from_q)
    done_q = finished(21, res_q, total(kept(gb_q)[:, x.a, x.p], s["intq"]))
    arrived(from_v2)
    s["vec"][...] = total(sumv[...], s["in2v"])
    arrived(done_d, done_u, done_q)
    left(swap_d, swap_u, swap_q, from_d, from_d2, from_u, from_u2, from_q, from_v, from_v2)
    left(done_d, done_u, done_q)
    store_out.wait()
    store_ing.wait()


def scratch(S, D, line, plane, rp):
    nb, n = S // QB, line * plane
    V = pltpu.VMEM
    shapes = dict(
        tok=V((S, D), BF), cot=V((S, D), BF), out=V((S, D), BF), ing=V((S, D), BF),
        large=pltpu.SemaphoreType.DMA((4,)), tile=V((16, D), F32), small=V((16, D), F32),
        wb=V((SLABS, line, plane, rp, D), BF),
        G=V((SLABS, D, D), F32), gs=V((16, D), F32),
        gq=V((2, line, plane, rp, D + 128), BF), inq=V((1, line, plane, rp, D + 128), BF),
        intq=V((n - 1, 1, rp, D + 128), BF), size=V((3, n, rp, D), BF),
        vectors=V((16, D), BF), inv=V((2 * plane - 1, 16, D), BF), sumv=V((16, D), BF), in2v=V((line - 1, 16, D), BF),
        inu=V((3, line, plane, rp, D), BF), in1u=V((plane - 1, 3, line, rp, D), BF),
        in2u=V((line - 1, 3, rp, D), BF), sumu=V((3, line, rp, D), BF),
        ind=V((2, line, plane, rp, D), BF), in1d=V((line - 1, 2, plane, rp, D), BF),
        in2d=V((plane - 1, 2, rp, D), BF), sumd=V((2, plane, rp, D), BF),
        mask=V((nb, QB, 2 * QB), F32), act=V((S, 128), F32), state=V((S, D), F32), mixed=V((S, D), F32),
        z1=V((2, S, D), F32), r1=V((2, S, 128), F32), n1=V((2, S, D), BF),
        z2=V((2, S, D), F32), r2=V((2, S, 128), F32), n2=V((2, S, D), BF),
        q=V((2, S, D), BF), k=V((2, S + QB, D), BF), v=V((2, S + QB, D), BF),
        p=V((2, nb, HEADS * QB, 2 * QB), BF), at=V((2, S, D), BF),
        h=V((2, 4, S, D), BF), d=V((2, 4, S, D), BF),
        bres=V((S, D), F32), do=V((S, D), BF),
        dq=V((S, D), BF), dk=V((S + QB, D), F32), dv=V((S + QB, D), F32), bi=V((S, D), F32),
    )
    if D // n != rp:
        shapes["wf"] = V((SLABS, D, D), BF)
    else:
        shapes["gb"] = V((10, line, plane, rp, D), BF)
    shapes["send"] = pltpu.SemaphoreType.DMA((25,))
    shapes["recv"] = pltpu.SemaphoreType.DMA((25,))
    return shapes


def finish(r, *refs):
    out_in, ing_in, res, resq, vec, out, ing, gq, gk, gv, go, gu, gd, gg1, gs1, gg2, gs2, gbu, gbd = refs
    out[...] = out_in[...]
    ing[...] = ing_in[...]
    D = res.shape[2]
    me = lax.axis_index("wide")
    gq[...] = resq[0, 0:r, 0:D]
    gk[...] = resq[1, 0:r, 0:D]
    for c in range(2):
        gv[:, 128 * c : 128 * (c + 1)] = resq[c, 0:r, D:]
    go[...] = res[0, 0:r, :]
    for c in range(4):
        gu[:, c * D : (c + 1) * D] = res[1 + c, 0:r, :]
        gd[:, c * D : (c + 1) * D] = res[6 + c, 0:r, :]
    tile = vec[...]
    own = pltpu.roll(tile, lax.rem(D - me * r, D), axis=1)
    for i, ref in enumerate((gg1, gs1, gg2, gs2, gbd)):
        ref[...] = own[i : i + 1, 0:r]
    row = jnp.zeros((1, D), F32)
    for c in range(4):
        row = jnp.where((me * 4 * r) // D == c, tile[5 + c : 6 + c, :], row)
    row = jnp.broadcast_to(row, (8, D))
    gbu[...] = pltpu.roll(row, lax.rem(D - lax.rem(me * 4 * r, D), D), axis=1)[0:1, 0 : 4 * r]


def on_device(sizes, *args):
    (tokens, lengths, counts, wq, wk, wv, wo, wu, wd, g1, s1, g2, s2, bu, bd, cot) = args
    line, plane = sizes
    S, D = tokens.shape[1:]
    r = wq.shape[0]
    rp = max(r, 16)
    vm = pl.BlockSpec(memory_space=pltpu.VMEM)
    hbm = pl.BlockSpec(memory_space=pl.ANY)
    inputs = dict(
        tok=tokens[0], cot=cot[0], lens=lengths, cnts=counts, wq=wq, wk=wk, wv=wv, wo=wo.T, up=wu, down=wd.T,
        g1=g1[None], s1=s1[None], g2=g2[None], s2=s2[None], bu=bu[None], bd=bd[None],
    )
    shapes = scratch(S, D, line, plane, rp)
    for key in FETCHED:
        space = pltpu.SMEM if key in ("lens", "cnts") else pltpu.VMEM
        shapes[key] = space(inputs[key].shape, inputs[key].dtype)
    shapes["fetch"] = pltpu.SemaphoreType.DMA((len(FETCHED),))
    names = [*(key + "_hbm" for key in inputs), "out_hbm", "ing_hbm", "res", "resq", "vec", *shapes]
    out, ing, res, resq, vec = pl.pallas_call(
        functools.partial(body, names, line, plane, r),
        out_shape=(
            jax.ShapeDtypeStruct((S, D), BF),
            jax.ShapeDtypeStruct((S, D), BF),
            jax.ShapeDtypeStruct((10, rp, D), F32),
            jax.ShapeDtypeStruct((2, rp, D + 128), F32),
            jax.ShapeDtypeStruct((16, D), F32),
        ),
        in_specs=[hbm] * len(inputs),
        out_specs=(hbm, hbm, vm, vm, vm),
        scratch_shapes=list(shapes.values()),
        compiler_params=pltpu.CompilerParams(
            collective_id=0, has_side_effects=True, vmem_limit_bytes=60 * 2**20
        ),
        name="loop_block",
    )(*inputs.values())
    f = lambda *shape: jax.ShapeDtypeStruct(shape, F32)
    out, ing, gq, gk, gv, go, gu, gd, gg1, gs1, gg2, gs2, gbu, gbd = pl.pallas_call(
        functools.partial(finish, r),
        out_shape=(
            jax.ShapeDtypeStruct((S, D), BF), jax.ShapeDtypeStruct((S, D), BF),
            f(r, D), f(r, D), f(r, D), f(r, D), f(r, 4 * D), f(r, 4 * D),
            f(1, r), f(1, r), f(1, r), f(1, r), f(1, 4 * r), f(1, r),
        ),
        in_specs=[vm] * 5,
        out_specs=(vm,) * 14,
        name="finish",
    )(out, ing, res, resq, vec)
    return (out[None], ing[None], gq, gk, gv, go.T, gu, gd.T, gg1[0], gs1[0], gg2[0], gs2[0], gbu[0], gbd[0])


def solution(mesh):
    wide = mesh.shape["wide"]
    line = 4 if wide % 4 == 0 else 1
    rows = P(("dp", "wide"), None, None)
    row = P(("dp", "wide"), None)
    first, second, one = P("wide", None), P(None, "wide"), P("wide")
    weights = (first, first, first, second, first, second)
    return jax.shard_map(
        functools.partial(on_device, (line, wide // line)),
        mesh=mesh,
        in_specs=(rows, row, row, *weights, *(one,) * 6, rows),
        out_specs=(rows, rows, *weights, *(one,) * 6),
        check_vma=False,
    )
```

```python
import functools
import math

import jax
import jax.numpy as jnp
from jax import lax
from jax.experimental import pallas as pl
from jax.experimental.pallas import tpu as pltpu
from jax.sharding import PartitionSpec as P

F32, BF = jnp.float32, jnp.bfloat16
MESH = pl.DeviceIdType.MESH
HEADS = 4
NORM_EPS = 1e-05
MASK_FILL = -1e30
QB = 128
NN = (((1,), (0,)), ((), ()))
NT = (((1,), (1,)), ((), ()))
TN = (((0,), (0,)), ((), ()))
C0 = math.sqrt(2 / math.pi)
C1 = C0 * 0.044715

SMALL, WQ, WK, WV, WO, WU, WD = 0, 1, 2, 3, 4, 5, 10
SLABS = 14
GROUP_A, GROUP_B, GROUP_C = (0, 2), (4, 3), (10, 2)


def dot(a, b, dims=NN):
    return lax.dot_general(a, b, dims, preferred_element_type=F32)


FETCHED = ("lens", "cnts", "wq", "wk", "wv", "wo", "up", "down", "g1", "s1", "g2", "s2", "bu", "bd")


class Exchange:
    def __init__(self, line, plane):
        self.line, self.plane = line, plane
        self.n = line * plane
        self.core = lax.axis_index("dp")
        self.me = lax.axis_index("wide")
        self.a = self.me // plane
        self.p = self.me % plane

    def chip(self, a, p):
        return {"dp": self.core, "wide": a * self.plane + p}

    def sibling(self):
        return {"dp": 1 - self.core, "wide": self.me}

    def along(self, step):
        return lax.rem(self.a + step, self.line)

    def across(self, step):
        return lax.rem(self.p + step, self.plane)


class Copies:
    def __init__(self, sems, k, size):
        self.send_sem, self.recv_sem, self.size = sems[0].at[k], sems[1].at[k], size

    def start(self, src, dst, device):
        pltpu.make_async_remote_copy(
            src_ref=src,
            dst_ref=dst,
            send_sem=self.send_sem,
            recv_sem=self.recv_sem,
            device_id=device,
            device_id_type=MESH,
        ).start()

    def arrived(self):
        pltpu.make_async_copy(self.size, self.size, self.recv_sem).wait()

    def left(self):
        pltpu.make_async_copy(self.size, self.size, self.send_sem).wait()


def arrived(*copies):
    for copy in copies:
        copy.arrived()


def left(*copies):
    for copy in copies:
        copy.left()


def layout(s):
    lens, cnts, G, gs = s["lens"], s["cnts"], s["G"], s["gs"]
    S, D = s["tok"].shape
    nb = S // QB
    slot = lax.broadcasted_iota(jnp.int32, (nb, QB), 0) * QB + lax.broadcasted_iota(jnp.int32, (nb, QB), 1)
    end = jnp.int32(0)
    start_of = jnp.zeros((nb, QB), jnp.int32)
    loops_of = jnp.zeros((nb, QB), jnp.int32)
    for j in range(lens.shape[1]):
        inside = slot >= end
        start_of = jnp.where(inside, end, start_of)
        loops_of = jnp.where(inside, cnts[0, j], loops_of)
        end = end + lens[0, j]
    start_t = jnp.transpose(start_of.astype(F32))
    loops_t = jnp.transpose(loops_of.astype(F32))
    kk = lax.broadcasted_iota(jnp.int32, (QB, 2 * QB), 1).astype(F32)
    qq = lax.broadcasted_iota(jnp.int32, (QB, 2 * QB), 0).astype(F32)
    for b in range(nb):
        ok = (kk >= start_t[:, b : b + 1] - (b - 1) * QB) & (kk <= qq + QB)
        if b == 0:
            ok = ok & (kk >= QB)
        s["mask"][b] = jnp.where(ok, 0.0, MASK_FILL)
        s["act"][pl.ds(b * QB, QB), :] = jnp.broadcast_to(
            jnp.where(loops_t[:, b : b + 1] > 1, 1.0, 0.0), (QB, 128)
        )
    for t in range(2):
        s["k"][t, 0:QB, :] = jnp.zeros((QB, D), BF)
        s["v"][t, 0:QB, :] = jnp.zeros((QB, D), BF)
    G[...] = jnp.zeros(G.shape, F32)
    gs[...] = jnp.zeros(gs.shape, F32)


def no_keys_ahead(s):
    for key in ("dk", "dv"):
        ref = s[key]
        ref[pl.ds(ref.shape[0] - QB, QB), :] = jnp.zeros((QB, ref.shape[1]), F32)


def block(s, W, C):
    tok, cot, out, ing, small, G, gs = (s[key] for key in ("tok", "cot", "out", "ing", "small", "G", "gs"))
    D = tok.shape[1]
    scale = (D // HEADS) ** -0.5
    lane_head = lax.broadcasted_iota(jnp.int32, (1, D), 1) // (D // HEADS)
    hm = [jnp.where(lane_head == h, 1.0, 0.0).astype(BF) for h in range(HEADS)]

    def wide(v):
        return jnp.concatenate([v, v], axis=1)

    def by_head(v):
        return jnp.concatenate([v * hm[h] for h in range(HEADS)], axis=0)

    def of_heads(v):
        own = v[0:QB]
        for h in range(1, HEADS):
            own = jnp.where(lane_head == h, v[h * QB : (h + 1) * QB], own)
        return own

    def block_rows(b):
        at = lambda k, size: pl.ds(pl.multiple_of(k * QB, QB), size)
        return at(b, 2 * QB), at(b, QB), at(b + 1, QB)

    def normalized(v):
        mean = jnp.mean(v, axis=1, keepdims=True)
        cen = v - mean
        var = jnp.mean(cen * cen, axis=1, keepdims=True)
        rstd = lax.rsqrt(var + NORM_EPS)
        return cen * rstd, jnp.broadcast_to(rstd, (C, 128))

    def add(ref, at, t, value):
        if t == 1 and C == tok.shape[0]:
            ref[at] = value
        else:
            ref[at] += value

    def forward_mixed(t, i):
        rows = pl.ds(pl.multiple_of(i * C, C), C)
        tk = tok[rows, :].astype(F32)
        mixed = tk + tk if t == 0 else s["state"][rows, :] + tk
        s["mixed"][rows, :] = mixed
        s["z1"][t, rows, :], s["r1"][t, rows, :] = normalized(mixed)

    def forward_attention(t, i):
        r0 = pl.multiple_of(i * C, C)
        rows = pl.ds(r0, C)
        n1 = (s["z1"][t, rows, :] * small[0:1, :] + small[1:2, :]).astype(BF)
        s["n1"][t, rows, :] = n1
        q = dot(n1, W(WQ)).astype(BF)
        s["q"][t, rows, :] = q
        s["k"][t, pl.ds(r0 + QB, C), :] = dot(n1, W(WK)).astype(BF)
        s["v"][t, pl.ds(r0 + QB, C), :] = dot(n1, W(WV)).astype(BF)
        for u in range(C // QB):
            b = i * (C // QB) + u
            win = pl.ds(pl.multiple_of(b * QB, QB), 2 * QB)
            kw, vw = s["k"][t, win, :], s["v"][t, win, :]
            qb = q[u * QB : (u + 1) * QB]
            sc = dot(by_head(qb), kw, NT)
            mask = s["mask"][b]
            ps = []
            for h in range(HEADS):
                e = sc[h * QB : (h + 1) * QB] * scale + mask
                e = jnp.exp(e - jnp.max(e, axis=1, keepdims=True))
                ps.append((e * (1.0 / jnp.sum(e, axis=1, keepdims=True))).astype(BF))
            p = jnp.concatenate(ps, axis=0)
            s["p"][t, b] = p
            s["at"][t, pl.ds(pl.multiple_of(b * QB, QB), QB), :] = of_heads(dot(p, vw)).astype(BF)

    def forward_hidden(t, i):
        rows = pl.ds(pl.multiple_of(i * C, C), C)
        resid = s["mixed"][rows, :] + dot(s["at"][t, rows, :], W(WO), NT)
        z2, s["r2"][t, rows, :] = normalized(resid)
        s["z2"][t, rows, :] = z2
        n2 = (z2 * small[2:3, :] + small[3:4, :]).astype(BF)
        s["n2"][t, rows, :] = n2
        acc = resid + small[4:5, :]
        for c in range(4):
            hp = dot(n2, W(WU + c)) + small[5 + c : 6 + c, :]
            v2 = hp * hp
            th = jnp.tanh(hp * (C1 * v2 + C0))
            pr = 0.5 * th + 0.5
            g = hp * pr
            d = pr + g * (1.0 - pr) * ((6 * C1) * v2 + (2 * C0))
            g = g.astype(BF)
            s["h"][t, c, rows, :] = g
            s["d"][t, c, rows, :] = d.astype(BF)
            acc = acc + dot(g, W(WD + c), NT)
        if t == 0:
            s["state"][rows, :] = acc
        else:
            act = wide(s["act"][rows, :])
            out[rows, :] = jnp.where(act > 0, acc, s["state"][rows, :]).astype(BF)

    def norm_bwd(t, dn, g, z, rstd, gi):
        e = dn * g
        add(gs, slice(gi, gi + 1), t, jnp.sum(dn * z, axis=0, keepdims=True))
        add(gs, slice(gi + 1, gi + 2), t, jnp.sum(dn, axis=0, keepdims=True))
        m1 = jnp.mean(e, axis=1, keepdims=True)
        m2 = jnp.mean(e * z, axis=1, keepdims=True)
        return wide(rstd) * (e - m1 - z * m2)

    def back_renewed(t, rows):
        if t == 0:
            return s["state"][rows, :]
        return jnp.where(wide(s["act"][rows, :]) > 0, cot[rows, :].astype(F32), 0.0)

    def backward_down(t, i):
        rows = pl.ds(pl.multiple_of(i * C, C), C)
        b2t = back_renewed(t, rows).astype(BF).T
        for c in range(4):
            add(G, WD + c, t, dot(b2t, s["h"][t, c, rows, :]))

    def backward_hidden(t, i):
        rows = pl.ds(pl.multiple_of(i * C, C), C)
        br = back_renewed(t, rows)
        add(gs, slice(4, 5), t, jnp.sum(br, axis=0, keepdims=True))
        b2 = br.astype(BF)
        n2t = s["n2"][t, rows, :].T
        dn2 = jnp.zeros((C, D), F32)
        for c in range(4):
            dp = s["d"][t, c, rows, :].astype(F32) * dot(b2, W(WD + c))
            add(gs, slice(5 + c, 6 + c), t, jnp.sum(dp, axis=0, keepdims=True))
            dp = dp.astype(BF)
            add(G, WU + c, t, dot(n2t, dp))
            dn2 = dn2 + dot(dp, W(WU + c), NT)
        bres = br + norm_bwd(t, dn2, small[2:3, :], s["z2"][t, rows, :], s["r2"][t, rows, :], 2)
        s["bres"][rows, :] = bres
        b1 = bres.astype(BF)
        add(G, WO, t, dot(b1.T, s["at"][t, rows, :]))
        s["do"][rows, :] = dot(b1, W(WO)).astype(BF)

    def backward_scores(t, i, blocks):
        for b in reversed(blocks):
            b = i * (C // QB) + b
            win, behind, ahead = block_rows(b)
            kw, vw = s["k"][t, win, :], s["v"][t, win, :]
            qs, dos = by_head(s["q"][t, behind, :]), by_head(s["do"][behind, :])
            p = s["p"][t, b]
            pf = p.astype(F32)
            tt = pf * dot(dos, vw, NT)
            ds = (tt - pf * jnp.sum(tt, axis=1, keepdims=True)).astype(BF)
            s["dq"][behind, :] = (of_heads(dot(ds, kw)) * scale).astype(BF)
            for ref, value in ((s["dv"], dot(p, dos, TN)), (s["dk"], dot(ds, qs, TN))):
                ref[behind, :] = value[0:QB]
                ref[ahead, :] += value[QB:]

    def backward_late(t, i):
        backward_scores(t, i, range(C // QB * 5 // 8, C // QB))

    def backward_early(t, i):
        backward_scores(t, i, range(C // QB * 5 // 8))
        rows = pl.ds(pl.multiple_of(i * C, C), C)
        own_keys = pl.ds(pl.multiple_of(i * C, C) + QB, C)
        n1t = s["n1"][t, rows, :].T
        add(G, WQ, t, dot(n1t, s["dq"][rows, :]))
        add(G, WK, t, dot(n1t, (s["dk"][own_keys, :] * scale).astype(BF)))
        add(G, WV, t, dot(n1t, s["dv"][own_keys, :].astype(BF)))

    def backward_mixed(t, i):
        r0 = pl.multiple_of(i * C, C)
        rows = pl.ds(r0, C)
        own_keys = pl.ds(r0 + QB, C)
        dn1 = dot(s["dq"][rows, :], W(WQ), NT)
        dn1 = dn1 + dot((s["dk"][own_keys, :] * scale).astype(BF), W(WK), NT)
        dn1 = dn1 + dot(s["dv"][own_keys, :].astype(BF), W(WV), NT)
        back = norm_bwd(t, dn1, small[0:1, :], s["z1"][t, rows, :], s["r1"][t, rows, :], 0)
        bm = s["bres"][rows, :] + back
        if t == 1:
            s["bi"][rows, :] = bm
            s["state"][rows, :] = jnp.where(wide(s["act"][rows, :]) > 0, 0.0, cot[rows, :].astype(F32)) + bm
        else:
            ing[rows, :] = (s["bi"][rows, :] + 2.0 * bm).astype(BF)

    forward = (forward_mixed, forward_attention, forward_hidden)
    return forward, (backward_down, backward_hidden, backward_late, backward_early, backward_mixed)


def body(names, line, plane, r, *refs):
    s = dict(zip(names, refs))
    res, wb, G, gs, small = s["res"], s["wb"], s["G"], s["gs"], s["small"]
    gb = s.get("gb", wb)
    S, D = s["tok"].shape
    n = line * plane
    rp = wb.shape[3]
    x = Exchange(line, plane)
    core, me = x.core, x.me

    large = s["large"]
    fetch_tok = pltpu.make_async_copy(s["tok_hbm"], s["tok"], large.at[0])
    fetch_cot = pltpu.make_async_copy(s["cot_hbm"], s["cot"], large.at[1])
    store_out = pltpu.make_async_copy(s["out"], s["out_hbm"], large.at[2])
    store_ing = pltpu.make_async_copy(s["ing"], s["ing_hbm"], large.at[3])
    barrier = pltpu.get_barrier_semaphore()
    pl.semaphore_signal(barrier, inc=1, device_id=x.sibling(), device_id_type=MESH)
    for k in range(1, n):
        pl.semaphore_signal(
            barrier,
            inc=1,
            device_id={"dp": core, "wide": lax.rem(me + k, n)},
            device_id_type=MESH,
        )

    fetches = [
        pltpu.make_async_copy(s[key + "_hbm"], s[key], s["fetch"].at[i]) for i, key in enumerate(FETCHED)
    ]
    for copy in (*fetches, fetch_tok, fetch_cot):
        copy.start()
    for copy in fetches:
        copy.wait()

    for k in range(1, plane):
        device = {"dp": 1 - core, "wide": x.chip(x.a, x.across(k))["wide"]}
        pl.semaphore_signal(barrier, inc=1, device_id=device, device_id_type=MESH)

    lanes = lax.broadcasted_iota(jnp.int32, (16, D), 1)
    rows16 = lax.broadcasted_iota(jnp.int32, (16, D), 0)
    tile = s["tile"]
    tile[...] = jnp.zeros((16, D), F32)
    for i, key in enumerate(("g1", "s1", "g2", "s2", "bd")):
        tile[i : i + 1, 0:r] = s[key][...].astype(F32)
    own = pltpu.roll(tile[...], me * r, axis=1)
    tile[0:1, 0 : 4 * r] = s["bu"][...].astype(F32)
    ups = jnp.broadcast_to(tile[0:1, :], (16, D))
    ups = jnp.where((lanes < 4 * r) & (rows16 == 5 + (me * 4 * r) // D), ups, 0.0)
    small_own = jnp.where(rows16 < 5, own, pltpu.roll(ups, lax.rem(me * 4 * r, D), axis=1)).astype(BF)
    first = jnp.where(core == 0, 1.0, 0.0).astype(BF)
    second = jnp.where(core == 0, 0.0, 1.0).astype(BF)

    def pad(v):
        return v if rp == r else jnp.concatenate([v.astype(F32), jnp.zeros((rp - r, D), F32)], axis=0).astype(BF)

    up = [pad(s["up"][:, c * D : (c + 1) * D]) for c in range(4)]
    down = [pad(s["down"][:, c * D : (c + 1) * D]) for c in range(4)]
    q_own, k_own, v_own, o_own = (pad(s[key][...]) for key in ("wq", "wk", "wv", "wo"))
    for (base, half), parts in (
        (GROUP_A, ((small_own, k_own), (q_own, v_own))),
        (GROUP_B, ((o_own, up[2]), (up[0], up[3]), (up[1], up[3]))),
        (GROUP_C, ((down[0], down[2]), (down[1], down[3]))),
    ):
        for i, (of_first, of_second) in enumerate(parts):
            wb[base + half * core + i, x.a, x.p] = of_first * first + of_second * second

    layout(s)

    def W(i):
        return wb[i].reshape(D, D) if rp == r else s["wf"][i]

    def places():
        row = lax.broadcasted_iota(jnp.int32, (D, n * rp), 0)
        place = lax.broadcasted_iota(jnp.int32, (D, n * rp), 1)
        return jnp.where(place == (row // r) * rp + lax.rem(row, r), 1.0, 0.0).astype(BF)

    def unpack(base, count):
        if rp != r:

            @pl.loop(base, base + count)
            def _(i):
                s["wf"][i] = dot(places(), wb[i].reshape(n * rp, D)).astype(BF)

    C = S if rp == r else 256
    forward, backward = block(s, W, C)
    forward_mixed, forward_attention, forward_hidden = forward
    backward_down, backward_hidden, backward_late, backward_early, backward_mixed = backward

    def chunks(t, *steps):
        def one(i):
            for step in steps:
                step(t, S // C - 1 - i if step in backward else i)

        if S == C:
            one(0)
        else:
            pl.loop(0, S // C)(one)

    fetch_tok.wait()
    chunks(0, forward_mixed)

    def mine(group):
        base, half = group
        return wb.at[pl.ds(base + half * core, half)]

    def start_all(k, size, sends):
        copies = Copies((s["send"], s["recv"]), k, size)
        for send in sends:
            copies.start(*send)
        return copies

    def along_line(k, size, ref, inbox):
        return start_all(k, size, [(ref(x.along(i)), inbox(i), x.chip(x.along(i), x.p)) for i in range(1, line)])

    def across_plane(k, size, ref, inbox):
        return start_all(k, size, [(ref(x.across(i)), inbox(i), x.chip(x.a, x.across(i))) for i in range(1, plane)])

    def to_sibling(k, size, src, dst):
        return start_all(k, size, [(src, dst, x.sibling())])

    def share(k, group):
        return to_sibling(k, mine(group), mine(group), mine(group))

    def bytes_of(group, devices):
        return s["size"].at[pl.ds(0, group[1]), pl.ds(0, devices)]

    pl.semaphore_wait(barrier, n + plane - 1)
    own_b, own_c = (mine(group).at[:, x.a, x.p] for group in (GROUP_B, GROUP_C))
    to_b = along_line(0, bytes_of(GROUP_B, line - 1), lambda _: own_b, lambda _: own_b)
    to_c = along_line(1, bytes_of(GROUP_C, line - 1), lambda _: own_c, lambda _: own_c)
    own_a = mine(GROUP_A).at[:, x.a, x.p]
    everyone = [{"dp": core, "wide": lax.rem(me + k, n)} for k in range(1, n)]
    to_a = start_all(2, bytes_of(GROUP_A, n - 1), [(own_a, own_a, device) for device in everyone])
    arrived(to_b)
    line_b, line_c = (mine(group).at[:, :, x.p] for group in (GROUP_B, GROUP_C))
    to_b2 = across_plane(3, bytes_of(GROUP_B, line * (plane - 1)), lambda _: line_b, lambda _: line_b)
    arrived(to_c)
    to_c2 = across_plane(4, bytes_of(GROUP_C, line * (plane - 1)), lambda _: line_c, lambda _: line_c)
    arrived(to_a)
    share_a = share(5, GROUP_A)
    arrived(share_a)
    small[...] = jnp.sum(wb[SMALL].reshape(n, rp, D).astype(F32), axis=0)[0:16]
    unpack(WQ, 3)
    chunks(0, forward_attention)
    arrived(to_b2)
    share_b = share(6, GROUP_B)
    arrived(to_c2)
    share_c = share(7, GROUP_C)
    arrived(share_b, share_c)
    unpack(WO, 5)
    unpack(WD, 4)
    chunks(0, forward_hidden)
    chunks(1, forward_mixed, forward_attention, forward_hidden)

    store_out.start()
    fetch_cot.wait()
    no_keys_ahead(s)
    chunks(1, *backward)

    def blocks(i):
        if rp == r:
            return G[i].astype(BF).reshape(line, plane, r, D)
        return dot(places(), G[i].astype(BF), TN).astype(BF).reshape(line, plane, rp, D)

    def stage(first_slab, *weights):
        for k, i in enumerate(weights):
            gb[first_slab + k] = blocks(i)

    def kept(ref):
        half = ref.shape[0] // 2
        return ref.at[pl.ds(half * core, half)]

    def swap(k, ref, inbox):
        half = ref.shape[0] // 2
        return to_sibling(k, inbox, ref.at[pl.ds(half * (1 - core), half)], inbox)

    def add_swapped(copies, ref, inbox):
        arrived(copies)
        own = kept(ref)

        def one(i):
            own[i] = (own[i].astype(F32) + inbox[i].astype(F32)).astype(BF)

        pl.loop(0, own.shape[0])(one)

    def total(own, inbox):
        own = own.astype(F32)
        for k in range(inbox.shape[0]):
            own = own + inbox[k].astype(F32)
        return own

    def finished(k, ref, sums):
        part = kept(ref)
        part[...] = sums
        return to_sibling(k, part, part, part)

    def straight(k, ref, inbox):
        sends = []
        for i in range(n - 1):
            to = i + jnp.where(i >= me, 1, 0)
            device = {"dp": core, "wide": to}
            sends.append((kept(ref).at[:, to // plane, lax.rem(to, plane)], inbox.at[me - jnp.where(me > to, 1, 0)], device))
        return start_all(k, inbox, sends)

    def summed(ref, own, inbox):
        ref[...] = total(own, inbox).astype(BF)
        return ref

    left(to_a, to_b, to_c, to_b2, to_c2, share_a, share_b, share_c)
    gb_u, gb_d, gb_q = gb.at[pl.ds(0, 4)], gb.at[pl.ds(4, 4)], s["gq"]
    res_q, res_u, res_d = s["resq"], res.at[pl.ds(0, 4)], res.at[pl.ds(4, 4)]

    def first_hop(k, ref, inbox):
        return across_plane(k, inbox, lambda p: kept(ref).at[:, :, p], lambda i: inbox.at[i - 1])

    def second_hop(k, sums, inbox):
        return along_line(k, inbox, lambda a: sums.at[:, a], lambda i: inbox.at[i - 1])

    chunks(0, backward_down)
    stage(4, WD, WD + 1, WD + 2, WD + 3)
    swap_d = swap(8, gb_d, s["ind"])
    chunks(0, backward_hidden)
    stage(0, WU, WU + 1, WU + 2, WU + 3)
    swap_u = swap(9, gb_u, s["inu"])
    add_swapped(swap_d, gb_d, s["ind"])
    from_d = first_hop(10, gb_d, s["in1d"])
    no_keys_ahead(s)
    if S == C:
        chunks(0, backward_late)
    add_swapped(swap_u, gb_u, s["inu"])
    from_u = first_hop(11, gb_u, s["in1u"])
    if S == C:
        chunks(0, backward_early)
    else:
        chunks(0, backward_late, backward_early)
    gb_q[0, :, :, :, 0:D] = blocks(WQ)
    gb_q[1, :, :, :, 0:D] = blocks(WK)
    for at, i in ((D, WV), (D + 128, WO)):
        halves = blocks(i)
        for c in range(2):
            gb_q[c, :, :, :, pl.ds(at, 128)] = halves[:, :, :, 128 * c : 128 * (c + 1)]
    swap_q = swap(15, gb_q, s["inq"])
    chunks(0, backward_mixed)
    store_ing.start()
    vectors = s["vectors"]
    vectors[...] = gs[...].astype(BF)
    near = [{"dp": other, "wide": x.chip(x.a, x.across(i))["wide"]} for other in (core, 1 - core) for i in range(plane)]
    from_v = start_all(23, s["inv"], [(vectors, s["inv"].at[i], device) for i, device in enumerate(near[1:])])
    arrived(from_d)
    sumd = summed(s["sumd"], kept(gb_d)[:, :, x.p], s["in1d"])
    from_d2 = second_hop(14, sumd, s["in2d"])
    add_swapped(swap_q, gb_q, s["inq"])
    from_q = first_hop(16, gb_q, s["in1q"])
    arrived(from_u)
    sumu = summed(s["sumu"], kept(gb_u)[:, :, x.p], s["in1u"])
    from_u2 = second_hop(17, sumu, s["in2u"])
    arrived(from_v)
    sumv = summed(s["sumv"], vectors[...], s["inv"])
    from_v2 = along_line(24, s["in2v"], lambda _: sumv, lambda i: s["in2v"].at[i - 1])
    arrived(from_q)
    sumq = summed(s["sumq"], kept(gb_q)[:, :, x.p], s["in1q"])
    from_q2 = second_hop(13, sumq, s["in2q"])
    arrived(from_d2)
    done_d = finished(18, res_d, total(sumd[:, x.a], s["in2d"]))
    arrived(from_u2)
    done_u = finished(20, res_u, total(sumu[:, x.a], s["in2u"]))
    arrived(from_v2)
    s["vec"][...] = total(sumv[...], s["in2v"])
    arrived(from_q2)
    done_q = finished(21, res_q, total(sumq[:, x.a], s["in2q"]))
    arrived(done_d, done_u, done_q)
    left(swap_d, swap_u, swap_q, from_d, from_d2, from_u, from_u2, from_q, from_q2, from_v, from_v2)
    left(done_d, done_u, done_q)
    store_out.wait()
    store_ing.wait()


def scratch(S, D, line, plane, rp):
    nb, n = S // QB, line * plane
    V = pltpu.VMEM
    shapes = dict(
        tok=V((S, D), BF), cot=V((S, D), BF), out=V((S, D), BF), ing=V((S, D), BF),
        large=pltpu.SemaphoreType.DMA((4,)), tile=V((16, D), F32), small=V((16, D), F32),
        wb=V((SLABS, line, plane, rp, D), BF),
        G=V((SLABS, D, D), F32), gs=V((16, D), F32),
        gq=V((2, line, plane, rp, 2 * D), BF), inq=V((1, line, plane, rp, 2 * D), BF),
        in1q=V((plane - 1, 1, line, rp, 2 * D), BF), in2q=V((line - 1, 1, rp, 2 * D), BF), sumq=V((1, line, rp, 2 * D), BF),
        size=V((3, n, rp, D), BF),
        vectors=V((16, D), BF), inv=V((2 * plane - 1, 16, D), BF), sumv=V((16, D), BF), in2v=V((line - 1, 16, D), BF),
        inu=V((2, line, plane, rp, D), BF), in1u=V((plane - 1, 2, line, rp, D), BF),
        in2u=V((line - 1, 2, rp, D), BF), sumu=V((2, line, rp, D), BF),
        ind=V((2, line, plane, rp, D), BF), in1d=V((plane - 1, 2, line, rp, D), BF),
        in2d=V((line - 1, 2, rp, D), BF), sumd=V((2, line, rp, D), BF),
        mask=V((nb, QB, 2 * QB), F32), act=V((S, 128), F32), state=V((S, D), F32), mixed=V((S, D), F32),
        z1=V((2, S, D), F32), r1=V((2, S, 128), F32), n1=V((2, S, D), BF),
        z2=V((2, S, D), F32), r2=V((2, S, 128), F32), n2=V((2, S, D), BF),
        q=V((2, S, D), BF), k=V((2, S + QB, D), BF), v=V((2, S + QB, D), BF),
        p=V((2, nb, HEADS * QB, 2 * QB), BF), at=V((2, S, D), BF),
        h=V((2, 4, S, D), BF), d=V((2, 4, S, D), BF),
        bres=V((S, D), F32), do=V((S, D), BF),
        dq=V((S, D), BF), dk=V((S + QB, D), F32), dv=V((S + QB, D), F32), bi=V((S, D), F32),
    )
    if D // n != rp:
        shapes["wf"] = V((SLABS, D, D), BF)
    else:
        shapes["gb"] = V((8, line, plane, rp, D), BF)
    shapes["send"] = pltpu.SemaphoreType.DMA((25,))
    shapes["recv"] = pltpu.SemaphoreType.DMA((25,))
    return shapes


def finish(r, *refs):
    out_in, ing_in, res, resq, vec, out, ing, gq, gk, gv, go, gu, gd, gg1, gs1, gg2, gs2, gbu, gbd = refs
    out[...] = out_in[...]
    ing[...] = ing_in[...]
    D = res.shape[2]
    me = lax.axis_index("wide")
    gq[...] = resq[0, 0:r, 0:D]
    gk[...] = resq[1, 0:r, 0:D]
    for c in range(2):
        half = slice(128 * c, 128 * (c + 1))
        gv[:, half] = resq[c, 0:r, D : D + 128]
        go[:, half] = resq[c, 0:r, D + 128 :]
    for c in range(4):
        gu[:, c * D : (c + 1) * D] = res[c, 0:r, :]
        gd[:, c * D : (c + 1) * D] = res[4 + c, 0:r, :]
    tile = vec[...]
    own = pltpu.roll(tile, lax.rem(D - me * r, D), axis=1)
    for i, ref in enumerate((gg1, gs1, gg2, gs2, gbd)):
        ref[...] = own[i : i + 1, 0:r]
    row = jnp.zeros((1, D), F32)
    for c in range(4):
        row = jnp.where((me * 4 * r) // D == c, tile[5 + c : 6 + c, :], row)
    row = jnp.broadcast_to(row, (8, D))
    gbu[...] = pltpu.roll(row, lax.rem(D - lax.rem(me * 4 * r, D), D), axis=1)[0:1, 0 : 4 * r]


def on_device(sizes, *args):
    (tokens, lengths, counts, wq, wk, wv, wo, wu, wd, g1, s1, g2, s2, bu, bd, cot) = args
    line, plane = sizes
    S, D = tokens.shape[1:]
    r = wq.shape[0]
    rp = max(r, 16)
    vm = pl.BlockSpec(memory_space=pltpu.VMEM)
    hbm = pl.BlockSpec(memory_space=pl.ANY)
    inputs = dict(
        tok=tokens[0], cot=cot[0], lens=lengths, cnts=counts, wq=wq, wk=wk, wv=wv, wo=wo.T, up=wu, down=wd.T,
        g1=g1[None], s1=s1[None], g2=g2[None], s2=s2[None], bu=bu[None], bd=bd[None],
    )
    shapes = scratch(S, D, line, plane, rp)
    for key in FETCHED:
        space = pltpu.SMEM if key in ("lens", "cnts") else pltpu.VMEM
        shapes[key] = space(inputs[key].shape, inputs[key].dtype)
    shapes["fetch"] = pltpu.SemaphoreType.DMA((len(FETCHED),))
    names = [*(key + "_hbm" for key in inputs), "out_hbm", "ing_hbm", "res", "resq", "vec", *shapes]
    out, ing, res, resq, vec = pl.pallas_call(
        functools.partial(body, names, line, plane, r),
        out_shape=(
            jax.ShapeDtypeStruct((S, D), BF),
            jax.ShapeDtypeStruct((S, D), BF),
            jax.ShapeDtypeStruct((8, rp, D), F32),
            jax.ShapeDtypeStruct((2, rp, 2 * D), F32),
            jax.ShapeDtypeStruct((16, D), F32),
        ),
        in_specs=[hbm] * len(inputs),
        out_specs=(hbm, hbm, vm, vm, vm),
        scratch_shapes=list(shapes.values()),
        compiler_params=pltpu.CompilerParams(
            collective_id=0, has_side_effects=True, vmem_limit_bytes=60 * 2**20
        ),
        name="loop_block",
    )(*inputs.values())
    f = lambda *shape: jax.ShapeDtypeStruct(shape, F32)
    out, ing, gq, gk, gv, go, gu, gd, gg1, gs1, gg2, gs2, gbu, gbd = pl.pallas_call(
        functools.partial(finish, r),
        out_shape=(
            jax.ShapeDtypeStruct((S, D), BF), jax.ShapeDtypeStruct((S, D), BF),
            f(r, D), f(r, D), f(r, D), f(r, D), f(r, 4 * D), f(r, 4 * D),
            f(1, r), f(1, r), f(1, r), f(1, r), f(1, 4 * r), f(1, r),
        ),
        in_specs=[vm] * 5,
        out_specs=(vm,) * 14,
        name="finish",
    )(out, ing, res, resq, vec)
    return (out[None], ing[None], gq, gk, gv, go.T, gu, gd.T, gg1[0], gs1[0], gg2[0], gs2[0], gbu[0], gbd[0])


def solution(mesh):
    wide = mesh.shape["wide"]
    line = 4 if wide % 4 == 0 else 1
    rows = P(("dp", "wide"), None, None)
    row = P(("dp", "wide"), None)
    first, second, one = P("wide", None), P(None, "wide"), P("wide")
    weights = (first, first, first, second, first, second)
    return jax.shard_map(
        functools.partial(on_device, (line, wide // line)),
        mesh=mesh,
        in_specs=(rows, row, row, *weights, *(one,) * 6, rows),
        out_specs=(rows, rows, *weights, *(one,) * 6),
        check_vma=False,
    )
```

```python
import functools
import math

import jax
import jax.numpy as jnp
from jax import lax
from jax.experimental import pallas as pl
from jax.experimental.pallas import tpu as pltpu
from jax.sharding import PartitionSpec as P

F32, BF = jnp.float32, jnp.bfloat16
MESH = pl.DeviceIdType.MESH
HEADS = 4
NORM_EPS = 1e-05
MASK_FILL = -1e30
QB = 128
NN = (((1,), (0,)), ((), ()))
NT = (((1,), (1,)), ((), ()))
TN = (((0,), (0,)), ((), ()))
C0 = math.sqrt(2 / math.pi)
C1 = C0 * 0.044715

SMALL, WQ, WK, WV, WO, WU, WD = 0, 1, 2, 3, 4, 5, 10
SLABS = 14
GROUP_A, GROUP_B, GROUP_C = (0, 2), (4, 3), (10, 2)


def dot(a, b, dims=NN):
    return lax.dot_general(a, b, dims, preferred_element_type=F32)


FETCHED = ("lens", "cnts", "wq", "wk", "wv", "wo", "up", "down", "g1", "s1", "g2", "s2", "bu", "bd")


class Exchange:
    def __init__(self, line, plane):
        self.line, self.plane = line, plane
        self.n = line * plane
        self.core = lax.axis_index("dp")
        self.me = lax.axis_index("wide")
        self.a = self.me // plane
        self.p = self.me % plane

    def chip(self, a, p):
        return {"dp": self.core, "wide": a * self.plane + p}

    def sibling(self):
        return {"dp": 1 - self.core, "wide": self.me}

    def along(self, step):
        return lax.rem(self.a + step, self.line)

    def across(self, step):
        return lax.rem(self.p + step, self.plane)


class Copies:
    def __init__(self, sems, k, size):
        self.send_sem, self.recv_sem, self.size = sems[0].at[k], sems[1].at[k], size

    def start(self, src, dst, device):
        pltpu.make_async_remote_copy(
            src_ref=src,
            dst_ref=dst,
            send_sem=self.send_sem,
            recv_sem=self.recv_sem,
            device_id=device,
            device_id_type=MESH,
        ).start()

    def arrived(self):
        pltpu.make_async_copy(self.size, self.size, self.recv_sem).wait()

    def left(self):
        pltpu.make_async_copy(self.size, self.size, self.send_sem).wait()


def arrived(*copies):
    for copy in copies:
        copy.arrived()


def left(*copies):
    for copy in copies:
        copy.left()


def layout(s):
    lens, cnts, G, gs = s["lens"], s["cnts"], s["G"], s["gs"]
    S, D = s["tok"].shape
    nb = S // QB
    slot = lax.broadcasted_iota(jnp.int32, (nb, QB), 0) * QB + lax.broadcasted_iota(jnp.int32, (nb, QB), 1)
    end = jnp.int32(0)
    start_of = jnp.zeros((nb, QB), jnp.int32)
    loops_of = jnp.zeros((nb, QB), jnp.int32)
    for j in range(lens.shape[1]):
        inside = slot >= end
        start_of = jnp.where(inside, end, start_of)
        loops_of = jnp.where(inside, cnts[0, j], loops_of)
        end = end + lens[0, j]
    start_t = jnp.transpose(start_of.astype(F32))
    loops_t = jnp.transpose(loops_of.astype(F32))
    kk = lax.broadcasted_iota(jnp.int32, (QB, 2 * QB), 1).astype(F32)
    qq = lax.broadcasted_iota(jnp.int32, (QB, 2 * QB), 0).astype(F32)
    for b in range(nb):
        ok = (kk >= start_t[:, b : b + 1] - (b - 1) * QB) & (kk <= qq + QB)
        if b == 0:
            ok = ok & (kk >= QB)
        s["mask"][b] = jnp.where(ok, 0.0, MASK_FILL)
        s["act"][pl.ds(b * QB, QB), :] = jnp.broadcast_to(
            jnp.where(loops_t[:, b : b + 1] > 1, 1.0, 0.0), (QB, 128)
        )
    for t in range(2):
        s["k"][t, 0:QB, :] = jnp.zeros((QB, D), BF)
        s["v"][t, 0:QB, :] = jnp.zeros((QB, D), BF)
    G[...] = jnp.zeros(G.shape, F32)
    gs[...] = jnp.zeros(gs.shape, F32)


def no_keys_ahead(s):
    for key in ("dk", "dv"):
        ref = s[key]
        ref[pl.ds(ref.shape[0] - QB, QB), :] = jnp.zeros((QB, ref.shape[1]), F32)


def block(s, W, C):
    tok, cot, out, ing, small, G, gs = (s[key] for key in ("tok", "cot", "out", "ing", "small", "G", "gs"))
    D = tok.shape[1]
    scale = (D // HEADS) ** -0.5
    lane_head = lax.broadcasted_iota(jnp.int32, (1, D), 1) // (D // HEADS)
    hm = [jnp.where(lane_head == h, 1.0, 0.0).astype(BF) for h in range(HEADS)]

    def wide(v):
        return jnp.concatenate([v, v], axis=1)

    def by_head(v):
        return jnp.concatenate([v * hm[h] for h in range(HEADS)], axis=0)

    def of_heads(v):
        own = v[0:QB]
        for h in range(1, HEADS):
            own = jnp.where(lane_head == h, v[h * QB : (h + 1) * QB], own)
        return own

    def block_rows(b):
        at = lambda k, size: pl.ds(pl.multiple_of(k * QB, QB), size)
        return at(b, 2 * QB), at(b, QB), at(b + 1, QB)

    def normalized(v):
        mean = jnp.mean(v, axis=1, keepdims=True)
        cen = v - mean
        var = jnp.mean(cen * cen, axis=1, keepdims=True)
        rstd = lax.rsqrt(var + NORM_EPS)
        return cen * rstd, jnp.broadcast_to(rstd, (C, 128))

    def add(ref, at, t, value):
        if t == 1 and C == tok.shape[0]:
            ref[at] = value
        else:
            ref[at] += value

    def forward_mixed(t, i):
        rows = pl.ds(pl.multiple_of(i * C, C), C)
        tk = tok[rows, :].astype(F32)
        mixed = tk + tk if t == 0 else s["state"][rows, :] + tk
        s["mixed"][rows, :] = mixed
        s["z1"][t, rows, :], s["r1"][t, rows, :] = normalized(mixed)

    def forward_attention(t, i):
        r0 = pl.multiple_of(i * C, C)
        rows = pl.ds(r0, C)
        n1 = (s["z1"][t, rows, :] * small[0:1, :] + small[1:2, :]).astype(BF)
        s["n1"][t, rows, :] = n1
        q = dot(n1, W(WQ)).astype(BF)
        s["q"][t, rows, :] = q
        s["k"][t, pl.ds(r0 + QB, C), :] = dot(n1, W(WK)).astype(BF)
        s["v"][t, pl.ds(r0 + QB, C), :] = dot(n1, W(WV)).astype(BF)
        for u in range(C // QB):
            b = i * (C // QB) + u
            win = pl.ds(pl.multiple_of(b * QB, QB), 2 * QB)
            kw, vw = s["k"][t, win, :], s["v"][t, win, :]
            qb = q[u * QB : (u + 1) * QB]
            sc = dot(by_head(qb), kw, NT)
            mask = s["mask"][b]
            ps = []
            for h in range(HEADS):
                e = sc[h * QB : (h + 1) * QB] * scale + mask
                e = jnp.exp(e - jnp.max(e, axis=1, keepdims=True))
                ps.append((e * (1.0 / jnp.sum(e, axis=1, keepdims=True))).astype(BF))
            p = jnp.concatenate(ps, axis=0)
            s["p"][t, b] = p
            s["at"][t, pl.ds(pl.multiple_of(b * QB, QB), QB), :] = of_heads(dot(p, vw)).astype(BF)

    def forward_hidden(t, i):
        rows = pl.ds(pl.multiple_of(i * C, C), C)
        resid = s["mixed"][rows, :] + dot(s["at"][t, rows, :], W(WO), NT)
        z2, s["r2"][t, rows, :] = normalized(resid)
        s["z2"][t, rows, :] = z2
        n2 = (z2 * small[2:3, :] + small[3:4, :]).astype(BF)
        s["n2"][t, rows, :] = n2
        acc = resid + small[4:5, :]
        for c in range(4):
            hp = dot(n2, W(WU + c)) + small[5 + c : 6 + c, :]
            v2 = hp * hp
            th = jnp.tanh(hp * (C1 * v2 + C0))
            pr = 0.5 * th + 0.5
            g = hp * pr
            d = pr + g * (1.0 - pr) * ((6 * C1) * v2 + (2 * C0))
            g = g.astype(BF)
            s["h"][t, c, rows, :] = g
            s["d"][t, c, rows, :] = d.astype(BF)
            acc = acc + dot(g, W(WD + c), NT)
        if t == 0:
            s["state"][rows, :] = acc
        else:
            act = wide(s["act"][rows, :])
            out[rows, :] = jnp.where(act > 0, acc, s["state"][rows, :]).astype(BF)

    def norm_bwd(t, dn, g, z, rstd, gi):
        e = dn * g
        add(gs, slice(gi, gi + 1), t, jnp.sum(dn * z, axis=0, keepdims=True))
        add(gs, slice(gi + 1, gi + 2), t, jnp.sum(dn, axis=0, keepdims=True))
        m1 = jnp.mean(e, axis=1, keepdims=True)
        m2 = jnp.mean(e * z, axis=1, keepdims=True)
        return wide(rstd) * (e - m1 - z * m2)

    def back_renewed(t, rows):
        if t == 0:
            return s["state"][rows, :]
        return jnp.where(wide(s["act"][rows, :]) > 0, cot[rows, :].astype(F32), 0.0)

    def backward_down(t, i):
        rows = pl.ds(pl.multiple_of(i * C, C), C)
        b2t = back_renewed(t, rows).astype(BF).T
        for c in range(4):
            add(G, WD + c, t, dot(b2t, s["h"][t, c, rows, :]))

    def backward_hidden(t, i):
        rows = pl.ds(pl.multiple_of(i * C, C), C)
        br = back_renewed(t, rows)
        add(gs, slice(4, 5), t, jnp.sum(br, axis=0, keepdims=True))
        b2 = br.astype(BF)
        n2t = s["n2"][t, rows, :].T
        dn2 = jnp.zeros((C, D), F32)
        for c in range(4):
            dp = s["d"][t, c, rows, :].astype(F32) * dot(b2, W(WD + c))
            add(gs, slice(5 + c, 6 + c), t, jnp.sum(dp, axis=0, keepdims=True))
            dp = dp.astype(BF)
            add(G, WU + c, t, dot(n2t, dp))
            dn2 = dn2 + dot(dp, W(WU + c), NT)
        bres = br + norm_bwd(t, dn2, small[2:3, :], s["z2"][t, rows, :], s["r2"][t, rows, :], 2)
        s["bres"][rows, :] = bres
        b1 = bres.astype(BF)
        add(G, WO, t, dot(b1.T, s["at"][t, rows, :]))
        s["do"][rows, :] = dot(b1, W(WO)).astype(BF)

    def backward_scores(t, i, blocks):
        for b in reversed(blocks):
            b = i * (C // QB) + b
            win, behind, ahead = block_rows(b)
            kw, vw = s["k"][t, win, :], s["v"][t, win, :]
            qs, dos = by_head(s["q"][t, behind, :]), by_head(s["do"][behind, :])
            p = s["p"][t, b]
            pf = p.astype(F32)
            tt = pf * dot(dos, vw, NT)
            ds = (tt - pf * jnp.sum(tt, axis=1, keepdims=True)).astype(BF)
            s["dq"][behind, :] = (of_heads(dot(ds, kw)) * scale).astype(BF)
            for ref, value in ((s["dv"], dot(p, dos, TN)), (s["dk"], dot(ds, qs, TN))):
                ref[behind, :] = value[0:QB]
                ref[ahead, :] += value[QB:]

    def backward_late(t, i):
        backward_scores(t, i, range(C // QB * 5 // 8, C // QB))

    def backward_early(t, i):
        backward_scores(t, i, range(C // QB * 5 // 8))
        rows = pl.ds(pl.multiple_of(i * C, C), C)
        own_keys = pl.ds(pl.multiple_of(i * C, C) + QB, C)
        n1t = s["n1"][t, rows, :].T
        add(G, WQ, t, dot(n1t, s["dq"][rows, :]))
        add(G, WK, t, dot(n1t, (s["dk"][own_keys, :] * scale).astype(BF)))
        add(G, WV, t, dot(n1t, s["dv"][own_keys, :].astype(BF)))

    def backward_mixed(t, i):
        r0 = pl.multiple_of(i * C, C)
        rows = pl.ds(r0, C)
        own_keys = pl.ds(r0 + QB, C)
        dn1 = dot(s["dq"][rows, :], W(WQ), NT)
        dn1 = dn1 + dot((s["dk"][own_keys, :] * scale).astype(BF), W(WK), NT)
        dn1 = dn1 + dot(s["dv"][own_keys, :].astype(BF), W(WV), NT)
        back = norm_bwd(t, dn1, small[0:1, :], s["z1"][t, rows, :], s["r1"][t, rows, :], 0)
        bm = s["bres"][rows, :] + back
        if t == 1:
            s["bi"][rows, :] = bm
            s["state"][rows, :] = jnp.where(wide(s["act"][rows, :]) > 0, 0.0, cot[rows, :].astype(F32)) + bm
        else:
            ing[rows, :] = (s["bi"][rows, :] + 2.0 * bm).astype(BF)

    forward = (forward_mixed, forward_attention, forward_hidden)
    return forward, (backward_down, backward_hidden, backward_late, backward_early, backward_mixed)


def body(names, line, plane, r, *refs):
    s = dict(zip(names, refs))
    res, wb, G, gs, small = s["res"], s["wb"], s["G"], s["gs"], s["small"]
    gb = s.get("gb", wb)
    S, D = s["tok"].shape
    n = line * plane
    rp = wb.shape[3]
    x = Exchange(line, plane)
    core, me = x.core, x.me

    large = s["large"]
    fetch_tok = pltpu.make_async_copy(s["tok_hbm"], s["tok"], large.at[0])
    fetch_cot = pltpu.make_async_copy(s["cot_hbm"], s["cot"], large.at[1])
    store_out = pltpu.make_async_copy(s["out"], s["out_hbm"], large.at[2])
    store_ing = pltpu.make_async_copy(s["ing"], s["ing_hbm"], large.at[3])
    barrier = pltpu.get_barrier_semaphore()
    pl.semaphore_signal(barrier, inc=1, device_id=x.sibling(), device_id_type=MESH)
    for k in range(1, n):
        pl.semaphore_signal(
            barrier,
            inc=1,
            device_id={"dp": core, "wide": lax.rem(me + k, n)},
            device_id_type=MESH,
        )

    fetches = [
        pltpu.make_async_copy(s[key + "_hbm"], s[key], s["fetch"].at[i]) for i, key in enumerate(FETCHED)
    ]
    for copy in (*fetches, fetch_tok, fetch_cot):
        copy.start()
    for copy in fetches:
        copy.wait()

    for k in range(1, plane):
        device = {"dp": 1 - core, "wide": x.chip(x.a, x.across(k))["wide"]}
        pl.semaphore_signal(barrier, inc=1, device_id=device, device_id_type=MESH)

    lanes = lax.broadcasted_iota(jnp.int32, (16, D), 1)
    rows16 = lax.broadcasted_iota(jnp.int32, (16, D), 0)
    tile = s["tile"]
    tile[...] = jnp.zeros((16, D), F32)
    for i, key in enumerate(("g1", "s1", "g2", "s2", "bd")):
        tile[i : i + 1, 0:r] = s[key][...].astype(F32)
    own = pltpu.roll(tile[...], me * r, axis=1)
    tile[0:1, 0 : 4 * r] = s["bu"][...].astype(F32)
    ups = jnp.broadcast_to(tile[0:1, :], (16, D))
    ups = jnp.where((lanes < 4 * r) & (rows16 == 5 + (me * 4 * r) // D), ups, 0.0)
    small_own = jnp.where(rows16 < 5, own, pltpu.roll(ups, lax.rem(me * 4 * r, D), axis=1)).astype(BF)
    first = jnp.where(core == 0, 1.0, 0.0).astype(BF)
    second = jnp.where(core == 0, 0.0, 1.0).astype(BF)

    def pad(v):
        return v if rp == r else jnp.concatenate([v.astype(F32), jnp.zeros((rp - r, D), F32)], axis=0).astype(BF)

    up = [pad(s["up"][:, c * D : (c + 1) * D]) for c in range(4)]
    down = [pad(s["down"][:, c * D : (c + 1) * D]) for c in range(4)]
    q_own, k_own, v_own, o_own = (pad(s[key][...]) for key in ("wq", "wk", "wv", "wo"))
    for (base, half), parts in (
        (GROUP_A, ((small_own, k_own), (q_own, v_own))),
        (GROUP_B, ((o_own, up[2]), (up[0], up[3]), (up[1], up[3]))),
        (GROUP_C, ((down[0], down[2]), (down[1], down[3]))),
    ):
        for i, (of_first, of_second) in enumerate(parts):
            wb[base + half * core + i, x.a, x.p] = of_first * first + of_second * second

    layout(s)

    def W(i):
        return wb[i].reshape(D, D) if rp == r else s["wf"][i]

    def places():
        row = lax.broadcasted_iota(jnp.int32, (D, n * rp), 0)
        place = lax.broadcasted_iota(jnp.int32, (D, n * rp), 1)
        return jnp.where(place == (row // r) * rp + lax.rem(row, r), 1.0, 0.0).astype(BF)

    def unpack(base, count):
        if rp != r:

            @pl.loop(base, base + count)
            def _(i):
                s["wf"][i] = dot(places(), wb[i].reshape(n * rp, D)).astype(BF)

    C = S if rp == r else 256
    forward, backward = block(s, W, C)
    forward_mixed, forward_attention, forward_hidden = forward
    backward_down, backward_hidden, backward_late, backward_early, backward_mixed = backward

    def chunks(t, *steps):
        def one(i):
            for step in steps:
                step(t, S // C - 1 - i if step in backward else i)

        if S == C:
            one(0)
        else:
            pl.loop(0, S // C)(one)

    fetch_tok.wait()
    chunks(0, forward_mixed)

    def mine(group):
        base, half = group
        return wb.at[pl.ds(base + half * core, half)]

    def start_all(k, size, sends):
        copies = Copies((s["send"], s["recv"]), k, size)
        for send in sends:
            copies.start(*send)
        return copies

    def along_line(k, size, ref, inbox):
        return start_all(k, size, [(ref(x.along(i)), inbox(i), x.chip(x.along(i), x.p)) for i in range(1, line)])

    def across_plane(k, size, ref, inbox, steps=range(1, plane)):
        return start_all(k, size, [(ref(x.across(i)), inbox(i), x.chip(x.a, x.across(i))) for i in steps])

    def to_sibling(k, size, src, dst):
        return start_all(k, size, [(src, dst, x.sibling())])

    def share(k, group):
        return to_sibling(k, mine(group), mine(group), mine(group))

    def bytes_of(group, devices):
        return s["size"].at[pl.ds(0, group[1]), pl.ds(0, devices)]

    pl.semaphore_wait(barrier, n + plane - 1)
    own_b, own_c = (mine(group).at[:, x.a, x.p] for group in (GROUP_B, GROUP_C))
    to_b = along_line(0, bytes_of(GROUP_B, line - 1), lambda _: own_b, lambda _: own_b)
    to_c = along_line(1, bytes_of(GROUP_C, line - 1), lambda _: own_c, lambda _: own_c)
    own_a = mine(GROUP_A).at[:, x.a, x.p]
    everyone = [{"dp": core, "wide": lax.rem(me + k, n)} for k in range(1, n)]
    to_a = start_all(2, bytes_of(GROUP_A, n - 1), [(own_a, own_a, device) for device in everyone])
    arrived(to_b)
    line_b, line_c = (mine(group).at[:, :, x.p] for group in (GROUP_B, GROUP_C))
    nearest_last = range(plane - 1, 0, -1)
    to_b2 = across_plane(3, bytes_of(GROUP_B, line * (plane - 1)), lambda _: line_b, lambda _: line_b, nearest_last)
    arrived(to_c)
    to_c2 = across_plane(4, bytes_of(GROUP_C, line * (plane - 1)), lambda _: line_c, lambda _: line_c, nearest_last)
    arrived(to_a)
    share_a = share(5, GROUP_A)
    arrived(share_a)
    small[...] = jnp.sum(wb[SMALL].reshape(n, rp, D).astype(F32), axis=0)[0:16]
    unpack(WQ, 3)
    chunks(0, forward_attention)
    arrived(to_b2)
    share_b = share(6, GROUP_B)
    arrived(to_c2)
    share_c = share(7, GROUP_C)
    arrived(share_b, share_c)
    unpack(WO, 5)
    unpack(WD, 4)
    chunks(0, forward_hidden)
    chunks(1, forward_mixed, forward_attention, forward_hidden)

    store_out.start()
    fetch_cot.wait()
    no_keys_ahead(s)
    chunks(1, *backward)

    def blocks(i):
        if rp == r:
            return G[i].astype(BF).reshape(line, plane, r, D)
        return dot(places(), G[i].astype(BF), TN).astype(BF).reshape(line, plane, rp, D)

    def stage(first_slab, *weights):
        for k, i in enumerate(weights):
            gb[first_slab + k] = blocks(i)

    def kept(ref):
        half = ref.shape[0] // 2
        return ref.at[pl.ds(half * core, half)]

    def swap(k, ref, inbox):
        half = ref.shape[0] // 2
        return to_sibling(k, inbox, ref.at[pl.ds(half * (1 - core), half)], inbox)

    def add_swapped(copies, ref, inbox):
        arrived(copies)
        own = kept(ref)

        def one(i):
            own[i] = (own[i].astype(F32) + inbox[i].astype(F32)).astype(BF)

        pl.loop(0, own.shape[0])(one)

    def total(own, inbox):
        own = own.astype(F32)
        for k in range(inbox.shape[0]):
            own = own + inbox[k].astype(F32)
        return own

    def finished(k, ref, sums):
        part = kept(ref)
        part[...] = sums
        return to_sibling(k, part, part, part)

    def straight(k, ref, inbox):
        sends = []
        for i in range(n - 1):
            to = i + jnp.where(i >= me, 1, 0)
            device = {"dp": core, "wide": to}
            sends.append((kept(ref).at[:, to // plane, lax.rem(to, plane)], inbox.at[me - jnp.where(me > to, 1, 0)], device))
        return start_all(k, inbox, sends)

    def summed(ref, own, inbox):
        ref[...] = total(own, inbox).astype(BF)
        return ref

    left(to_a, to_b, to_c, to_b2, to_c2, share_a, share_b, share_c)
    gb_u, gb_d, gb_q = gb.at[pl.ds(0, 4)], gb.at[pl.ds(4, 4)], s["gq"]
    res_q, res_u, res_d = s["resq"], res.at[pl.ds(0, 4)], res.at[pl.ds(4, 4)]

    def first_hop(k, ref, inbox):
        return across_plane(k, inbox, lambda p: kept(ref).at[:, :, p], lambda i: inbox.at[i - 1])

    def second_hop(k, sums, inbox):
        return along_line(k, inbox, lambda a: sums.at[:, a], lambda i: inbox.at[i - 1])

    chunks(0, backward_down)
    stage(4, WD, WD + 1, WD + 2, WD + 3)
    swap_d = swap(8, gb_d, s["ind"])
    chunks(0, backward_hidden)
    stage(0, WU, WU + 1, WU + 2, WU + 3)
    swap_u = swap(9, gb_u, s["inu"])
    add_swapped(swap_d, gb_d, s["ind"])
    from_d = first_hop(10, gb_d, s["in1d"])
    no_keys_ahead(s)
    if S == C:
        chunks(0, backward_late)
    add_swapped(swap_u, gb_u, s["inu"])
    from_u = first_hop(11, gb_u, s["in1u"])
    if S == C:
        chunks(0, backward_early)
    else:
        chunks(0, backward_late, backward_early)
    gb_q[0, :, :, :, 0:D] = blocks(WQ)
    gb_q[1, :, :, :, 0:D] = blocks(WK)
    for at, i in ((D, WV), (D + 128, WO)):
        halves = blocks(i)
        for c in range(2):
            gb_q[c, :, :, :, pl.ds(at, 128)] = halves[:, :, :, 128 * c : 128 * (c + 1)]
    swap_q = swap(15, gb_q, s["inq"])
    chunks(0, backward_mixed)
    store_ing.start()
    vectors = s["vectors"]
    vectors[...] = gs[...].astype(BF)
    near = [{"dp": other, "wide": x.chip(x.a, x.across(i))["wide"]} for other in (core, 1 - core) for i in range(plane)]
    from_v = start_all(23, s["inv"], [(vectors, s["inv"].at[i], device) for i, device in enumerate(near[1:])])
    arrived(from_d)
    sumd = summed(s["sumd"], kept(gb_d)[:, :, x.p], s["in1d"])
    from_d2 = second_hop(14, sumd, s["in2d"])
    add_swapped(swap_q, gb_q, s["inq"])
    from_q = first_hop(16, gb_q, s["in1q"])
    arrived(from_u)
    sumu = summed(s["sumu"], kept(gb_u)[:, :, x.p], s["in1u"])
    from_u2 = second_hop(17, sumu, s["in2u"])
    arrived(from_v)
    sumv = summed(s["sumv"], vectors[...], s["inv"])
    from_v2 = along_line(24, s["in2v"], lambda _: sumv, lambda i: s["in2v"].at[i - 1])
    arrived(from_q)
    sumq = summed(s["sumq"], kept(gb_q)[:, :, x.p], s["in1q"])
    from_q2 = second_hop(13, sumq, s["in2q"])
    arrived(from_d2)
    done_d = finished(18, res_d, total(sumd[:, x.a], s["in2d"]))
    arrived(from_u2)
    done_u = finished(20, res_u, total(sumu[:, x.a], s["in2u"]))
    arrived(from_v2)
    s["vec"][...] = total(sumv[...], s["in2v"])
    arrived(from_q2)
    done_q = finished(21, res_q, total(sumq[:, x.a], s["in2q"]))
    arrived(done_d, done_u, done_q)
    left(swap_d, swap_u, swap_q, from_d, from_d2, from_u, from_u2, from_q, from_q2, from_v, from_v2)
    left(done_d, done_u, done_q)
    store_out.wait()
    store_ing.wait()


def scratch(S, D, line, plane, rp):
    nb, n = S // QB, line * plane
    V = pltpu.VMEM
    shapes = dict(
        tok=V((S, D), BF), cot=V((S, D), BF), out=V((S, D), BF), ing=V((S, D), BF),
        large=pltpu.SemaphoreType.DMA((4,)), tile=V((16, D), F32), small=V((16, D), F32),
        wb=V((SLABS, line, plane, rp, D), BF),
        G=V((SLABS, D, D), F32), gs=V((16, D), F32),
        gq=V((2, line, plane, rp, 2 * D), BF), inq=V((1, line, plane, rp, 2 * D), BF),
        in1q=V((plane - 1, 1, line, rp, 2 * D), BF), in2q=V((line - 1, 1, rp, 2 * D), BF), sumq=V((1, line, rp, 2 * D), BF),
        size=V((3, n, rp, D), BF),
        vectors=V((16, D), BF), inv=V((2 * plane - 1, 16, D), BF), sumv=V((16, D), BF), in2v=V((line - 1, 16, D), BF),
        inu=V((2, line, plane, rp, D), BF), in1u=V((plane - 1, 2, line, rp, D), BF),
        in2u=V((line - 1, 2, rp, D), BF), sumu=V((2, line, rp, D), BF),
        ind=V((2, line, plane, rp, D), BF), in1d=V((plane - 1, 2, line, rp, D), BF),
        in2d=V((line - 1, 2, rp, D), BF), sumd=V((2, line, rp, D), BF),
        mask=V((nb, QB, 2 * QB), F32), act=V((S, 128), F32), state=V((S, D), F32), mixed=V((S, D), F32),
        z1=V((2, S, D), F32), r1=V((2, S, 128), F32), n1=V((2, S, D), BF),
        z2=V((2, S, D), F32), r2=V((2, S, 128), F32), n2=V((2, S, D), BF),
        q=V((2, S, D), BF), k=V((2, S + QB, D), BF), v=V((2, S + QB, D), BF),
        p=V((2, nb, HEADS * QB, 2 * QB), BF), at=V((2, S, D), BF),
        h=V((2, 4, S, D), BF), d=V((2, 4, S, D), BF),
        bres=V((S, D), F32), do=V((S, D), BF),
        dq=V((S, D), BF), dk=V((S + QB, D), F32), dv=V((S + QB, D), F32), bi=V((S, D), F32),
    )
    if D // n != rp:
        shapes["wf"] = V((SLABS, D, D), BF)
    else:
        shapes["gb"] = V((8, line, plane, rp, D), BF)
    shapes["send"] = pltpu.SemaphoreType.DMA((25,))
    shapes["recv"] = pltpu.SemaphoreType.DMA((25,))
    return shapes


def finish(r, *refs):
    out_in, ing_in, res, resq, vec, out, ing, gq, gk, gv, go, gu, gd, gg1, gs1, gg2, gs2, gbu, gbd = refs
    out[...] = out_in[...]
    ing[...] = ing_in[...]
    D = res.shape[2]
    me = lax.axis_index("wide")
    gq[...] = resq[0, 0:r, 0:D]
    gk[...] = resq[1, 0:r, 0:D]
    for c in range(2):
        half = slice(128 * c, 128 * (c + 1))
        gv[:, half] = resq[c, 0:r, D : D + 128]
        go[:, half] = resq[c, 0:r, D + 128 :]
    for c in range(4):
        gu[:, c * D : (c + 1) * D] = res[c, 0:r, :]
        gd[:, c * D : (c + 1) * D] = res[4 + c, 0:r, :]
    tile = vec[...]
    own = pltpu.roll(tile, lax.rem(D - me * r, D), axis=1)
    for i, ref in enumerate((gg1, gs1, gg2, gs2, gbd)):
        ref[...] = own[i : i + 1, 0:r]
    row = jnp.zeros((1, D), F32)
    for c in range(4):
        row = jnp.where((me * 4 * r) // D == c, tile[5 + c : 6 + c, :], row)
    row = jnp.broadcast_to(row, (8, D))
    gbu[...] = pltpu.roll(row, lax.rem(D - lax.rem(me * 4 * r, D), D), axis=1)[0:1, 0 : 4 * r]


def on_device(sizes, *args):
    (tokens, lengths, counts, wq, wk, wv, wo, wu, wd, g1, s1, g2, s2, bu, bd, cot) = args
    line, plane = sizes
    S, D = tokens.shape[1:]
    r = wq.shape[0]
    rp = max(r, 16)
    vm = pl.BlockSpec(memory_space=pltpu.VMEM)
    hbm = pl.BlockSpec(memory_space=pl.ANY)
    inputs = dict(
        tok=tokens[0], cot=cot[0], lens=lengths, cnts=counts, wq=wq, wk=wk, wv=wv, wo=wo.T, up=wu, down=wd.T,
        g1=g1[None], s1=s1[None], g2=g2[None], s2=s2[None], bu=bu[None], bd=bd[None],
    )
    shapes = scratch(S, D, line, plane, rp)
    for key in FETCHED:
        space = pltpu.SMEM if key in ("lens", "cnts") else pltpu.VMEM
        shapes[key] = space(inputs[key].shape, inputs[key].dtype)
    shapes["fetch"] = pltpu.SemaphoreType.DMA((len(FETCHED),))
    names = [*(key + "_hbm" for key in inputs), "out_hbm", "ing_hbm", "res", "resq", "vec", *shapes]
    out, ing, res, resq, vec = pl.pallas_call(
        functools.partial(body, names, line, plane, r),
        out_shape=(
            jax.ShapeDtypeStruct((S, D), BF),
            jax.ShapeDtypeStruct((S, D), BF),
            jax.ShapeDtypeStruct((8, rp, D), F32),
            jax.ShapeDtypeStruct((2, rp, 2 * D), F32),
            jax.ShapeDtypeStruct((16, D), F32),
        ),
        in_specs=[hbm] * len(inputs),
        out_specs=(hbm, hbm, vm, vm, vm),
        scratch_shapes=list(shapes.values()),
        compiler_params=pltpu.CompilerParams(
            collective_id=0, has_side_effects=True, vmem_limit_bytes=60 * 2**20
        ),
        name="loop_block",
    )(*inputs.values())
    f = lambda *shape: jax.ShapeDtypeStruct(shape, F32)
    out, ing, gq, gk, gv, go, gu, gd, gg1, gs1, gg2, gs2, gbu, gbd = pl.pallas_call(
        functools.partial(finish, r),
        out_shape=(
            jax.ShapeDtypeStruct((S, D), BF), jax.ShapeDtypeStruct((S, D), BF),
            f(r, D), f(r, D), f(r, D), f(r, D), f(r, 4 * D), f(r, 4 * D),
            f(1, r), f(1, r), f(1, r), f(1, r), f(1, 4 * r), f(1, r),
        ),
        in_specs=[vm] * 5,
        out_specs=(vm,) * 14,
        name="finish",
    )(out, ing, res, resq, vec)
    return (out[None], ing[None], gq, gk, gv, go.T, gu, gd.T, gg1[0], gs1[0], gg2[0], gs2[0], gbu[0], gbd[0])


def solution(mesh):
    wide = mesh.shape["wide"]
    line = 4 if wide % 4 == 0 else 1
    rows = P(("dp", "wide"), None, None)
    row = P(("dp", "wide"), None)
    first, second, one = P("wide", None), P(None, "wide"), P("wide")
    weights = (first, first, first, second, first, second)
    return jax.shard_map(
        functools.partial(on_device, (line, wide // line)),
        mesh=mesh,
        in_specs=(rows, row, row, *weights, *(one,) * 6, rows),
        out_specs=(rows, rows, *weights, *(one,) * 6),
        check_vma=False,
    )
```
